128 devices in a mesh: blk: 8 (over x, z_hi), grp: 16 (over z_lo, y, core).
Axes of the slice: x: 4, y: 4, z: 4 (z_hi: 2, z_lo: 2; z = z_hi * 2 + z_lo), core: 2. Of those that a mesh axis runs over, the one named last changes fastest.
Arguments:
- first_pooled_view: bfloat16 [16384, 4096], P(('blk', 'grp')), may hold values from -0.25 to 0.25
- second_pooled_view: bfloat16 [16384, 4096], P(('blk', 'grp')), may hold values from -0.25 to 0.25
- partner: int32 [128, 128], P(('blk', 'grp')), may hold values from 0 to 127, as said below
- adapter_down_weight: bfloat16 [4096, 64], replicated, may hold values from -0.09375 to 0.09375
- adapter_up_weight: bfloat16 [64, 1024], replicated, may hold values from -0.75 to 0.75
Outputs:
- loss: float32 [], replicated
- first_view_gradient: bfloat16 [16384, 4096], P(('blk', 'grp'))
- second_view_gradient: bfloat16 [16384, 4096], P(('blk', 'grp'))
- grad_down: float32 [4096, 64], replicated
- grad_up: float32 [64, 1024], replicated
The draws below stay inside these ranges and needn't reach their ends.
Inputs may be any that keep to these rules, and one draw needn't show every extreme that they name: Each row of partner is a permutation of 0 to 127.
All inputs are finite; a program needn't handle non-finite values.
Results may differ from the reference program's by a relative error of at most 0.0076.
Values may be sent and summed in bfloat16 or wider, within the bound.
A program may use at most 192 MiB of HBM per device.

```python
import math
import jax
import jax.numpy as jnp
from jax import lax

MODEL_WIDTH = 4096
KEPT_WIDTH = 1024
ADAPTER_RANK = 64
ROWS = 128
N_TEXTS = 16384


def pair_rows(key):
    block_keys = jax.random.split(jax.random.fold_in(key, 101), N_TEXTS // ROWS)

    def one_block(block_key):
        return jax.random.permutation(block_key, ROWS)
    return jax.vmap(one_block)(block_keys).astype(jnp.int32)


def paired_views(key, low_share, high_share):
    partner_rows = pair_rows(key)
    group_count = max(2, N_TEXTS // 1024)
    member_key, share_key, center_key, own_key, noise_key, close_key = jax.random.split(jax.random.fold_in(key, 202), 6)
    members = jax.random.randint(member_key, (N_TEXTS,), 0, group_count)
    center_share = jax.random.uniform(share_key, (N_TEXTS, 1), jnp.float32, low_share, high_share)
    centers = jax.random.normal(center_key, (group_count, MODEL_WIDTH), jnp.float32)
    own_part = jax.random.normal(own_key, (N_TEXTS, MODEL_WIDTH), jnp.float32)
    first_view = jnp.sqrt(center_share) * centers[members] + jnp.sqrt(1.0 - center_share) * own_part
    closeness = jax.random.uniform(close_key, (N_TEXTS, 1), jnp.float32, 0.6, 0.85)
    fresh_noise = jax.random.normal(noise_key, (N_TEXTS, MODEL_WIDTH), jnp.float32)
    second_rows = closeness * first_view + jnp.sqrt(1.0 - closeness * closeness) * fresh_noise
    offsets = (jnp.arange(N_TEXTS // ROWS, dtype=jnp.int32) * ROWS)[:, None]
    pair_target = (partner_rows + offsets).reshape(-1)
    second_view = jnp.zeros((N_TEXTS, MODEL_WIDTH), jnp.float32).at[pair_target].set(second_rows)
    return (first_view, second_view)


def draw_partner(key, part):
    return pair_rows(key)


def draw_first_pooled_view(key, part):
    first_view, second_view = paired_views(key, 0.45, 0.85)
    return jnp.clip(0.03125 * first_view, -0.25, 0.25).astype(jnp.bfloat16)


def draw_second_pooled_view(key, part):
    first_view, second_view = paired_views(key, 0.45, 0.85)
    return jnp.clip(0.03125 * second_view, -0.25, 0.25).astype(jnp.bfloat16)


def scatter_about(rng, dims, deviation, reach, kind=jnp.bfloat16):
    result = jax.random.normal(rng, dims, jnp.float32) * deviation
    return jnp.minimum(jnp.maximum(result, -reach), reach).astype(kind)


def setup_inputs(seed: int = 0) -> dict:
    keys = jax.random.split(jax.random.key(seed), 6)
    first_pooled_view = draw_first_pooled_view(jax.random.fold_in(keys[5], 71), 0)
    second_pooled_view = draw_second_pooled_view(jax.random.fold_in(keys[5], 71), 0)
    partner = draw_partner(jax.random.fold_in(keys[5], 71), 0)
    adapter_down_weight = scatter_about(keys[3], (MODEL_WIDTH, ADAPTER_RANK), MODEL_WIDTH ** -0.5, 0.09375)
    adapter_up_weight = scatter_about(keys[4], (ADAPTER_RANK, KEPT_WIDTH), ADAPTER_RANK ** -0.5, 0.75)
    return dict(first_pooled_view=first_pooled_view, second_pooled_view=second_pooled_view, partner=partner, adapter_down_weight=adapter_down_weight, adapter_up_weight=adapter_up_weight)


SCALE = 20.0
EPS = 1e-06

def embed_texts(hidden_states, adapter_down_weight, adapter_up_weight):
    reduced_projection = jnp.dot(hidden_states, adapter_down_weight, preferred_element_type=jnp.float32).astype(jnp.bfloat16)
    combined_states = hidden_states[:, :KEPT_WIDTH].astype(jnp.float32) + jnp.dot(reduced_projection, adapter_up_weight, preferred_element_type=jnp.float32)
    inverse_norm = lax.rsqrt(lax.optimization_barrier(jnp.sum(combined_states * combined_states, axis=1, keepdims=True)) + EPS)
    return (reduced_projection, combined_states * inverse_norm, inverse_norm)

def adapter_backward(hidden_states, reduced_projection, normalized_rows, inverse_norm, normalized_gradient, adapter_down_weight, adapter_up_weight):
    grad_mixed = inverse_norm * (normalized_gradient - normalized_rows * lax.optimization_barrier(jnp.sum(normalized_rows * normalized_gradient, axis=1, keepdims=True)))
    half_gradient = lax.optimization_barrier(grad_mixed.astype(jnp.bfloat16))
    reduced_gradient = jnp.dot(half_gradient, adapter_up_weight.T, preferred_element_type=jnp.float32).astype(jnp.bfloat16)
    padded_states = jnp.pad(half_gradient.astype(jnp.float32), ((0, 0), (0, hidden_states.shape[1] - half_gradient.shape[1])))
    state_gradient = (padded_states + jnp.dot(reduced_gradient, adapter_down_weight.T, preferred_element_type=jnp.float32)).astype(jnp.bfloat16)
    down_term = jnp.dot(hidden_states.T, reduced_gradient, preferred_element_type=jnp.float32)
    up_term = jnp.dot(reduced_projection.T, half_gradient, preferred_element_type=jnp.float32)
    return (state_gradient, down_term, up_term)

def reference(first_pooled_view, second_pooled_view, partner, adapter_down_weight, adapter_up_weight):
    first_reduced, first_normalized, first_inverse_norm = embed_texts(first_pooled_view, adapter_down_weight, adapter_up_weight)
    second_reduced, second_normalized, second_inverse_norm = embed_texts(second_pooled_view, adapter_down_weight, adapter_up_weight)
    query_units = first_normalized.astype(jnp.bfloat16)
    key_units = second_normalized.astype(jnp.bfloat16)
    text_count = query_units.shape[0]
    offsets = (jnp.arange(partner.shape[0], dtype=jnp.int32) * ROWS)[:, None]
    target = (partner + offsets).reshape(-1).astype(jnp.int32)
    block_rows = math.gcd(text_count, 1024)
    nblocks = text_count // block_rows
    query_blocks = query_units.reshape(nblocks, block_rows, KEPT_WIDTH)

    def forward(col_acc, query_block):
        exps_tile = jnp.exp(SCALE * jnp.dot(query_block, key_units.T, preferred_element_type=jnp.float32) - SCALE)
        return (col_acc + lax.optimization_barrier(jnp.sum(exps_tile, axis=0)), lax.optimization_barrier(jnp.sum(exps_tile, axis=1)))
    col_total, row_total = lax.scan(forward, jnp.zeros((text_count,), jnp.float32), query_blocks)
    row_total = row_total.reshape(-1)
    pos_keys = key_units[target].astype(jnp.float32)
    positive = SCALE * lax.optimization_barrier(jnp.sum(query_units.astype(jnp.float32) * pos_keys, axis=1))
    loss = (0.5 * jnp.sum(jnp.log(row_total)) + 0.5 * jnp.sum(jnp.log(col_total))) / text_count + SCALE - jnp.sum(positive) / text_count
    inv_col = 1.0 / col_total

    def backward(key_acc, inputs):
        query_block, row_block = inputs
        exps_tile = jnp.exp(SCALE * jnp.dot(query_block, key_units.T, preferred_element_type=jnp.float32) - SCALE)
        weights = (0.5 * exps_tile * (1.0 / row_block[:, None] + inv_col[None, :])).astype(jnp.bfloat16)
        query_grad = jnp.dot(weights, key_units, preferred_element_type=jnp.float32)
        key_acc = key_acc + jnp.dot(weights.T, query_block, preferred_element_type=jnp.float32)
        return (key_acc, query_grad)
    key_sum, query_sum = lax.scan(backward, jnp.zeros((text_count, KEPT_WIDTH), jnp.float32), (query_blocks, row_total.reshape(nblocks, block_rows)))
    query_sum = query_sum.reshape(text_count, KEPT_WIDTH)
    pos_queries = jnp.zeros((text_count, KEPT_WIDTH), jnp.float32).at[target].add(query_units.astype(jnp.float32))
    query_gradient = SCALE * (query_sum - pos_keys)
    key_gradient = SCALE * (key_sum - pos_queries)
    first_view_gradient, first_down_product, first_up_product = adapter_backward(first_pooled_view, first_reduced, first_normalized, first_inverse_norm, query_gradient, adapter_down_weight, adapter_up_weight)
    second_view_gradient, second_down_product, second_up_product = adapter_backward(second_pooled_view, second_reduced, second_normalized, second_inverse_norm, key_gradient, adapter_down_weight, adapter_up_weight)
    return (loss, first_view_gradient, second_view_gradient, first_down_product + second_down_product, first_up_product + second_up_product)
```

```python
import jax
import jax.numpy as jnp
from jax import lax
from jax.experimental import pallas as pl
from jax.experimental.pallas import tpu as pltpu
from jax.sharding import PartitionSpec as P

SCALE = 20.0
EPS = 1e-06
MESH = pl.DeviceIdType.MESH
F32 = jnp.float32
BF16 = jnp.bfloat16

ROWS = 128
WIDTH = 1024
MODEL = 4096
RANK = 64
LANES = 128
TEXTS = 16384

OWN, UP, DOWN, PAIR, FAR, UP_PAIR, DOWN_PAIR, FAR_PAIR = range(8)
PLACE = {OWN: (0, 0), UP: (1, 0), DOWN: (3, 0), PAIR: (0, 1), FAR: (2, 0), UP_PAIR: (1, 1), DOWN_PAIR: (3, 1), FAR_PAIR: (2, 1)}
SLOT = {place: slot for slot, place in PLACE.items()}
HALF = ROWS // 2
COPIES = 160


def nn(a, b):
    return lax.dot_general(a, b, (((1,), (0,)), ((), ())), preferred_element_type=F32)


def nt(a, b):
    return lax.dot_general(a, b, (((1,), (1,)), ((), ())), preferred_element_type=F32)


def tn(a, b):
    return lax.dot_general(a, b, (((0,), (0,)), ((), ())), preferred_element_type=F32)


class Links:
    def __init__(self, send_sems, recv_sems):
        self.send_sems, self.recv_sems, self.count, self.sent = send_sems, recv_sems, 0, []

    def copy(self, src, dst, device):
        index = self.count
        self.count += 1
        made = pltpu.make_async_remote_copy(
            src_ref=src,
            dst_ref=dst,
            send_sem=self.send_sems.at[index],
            recv_sem=self.recv_sems.at[index],
            device_id=device,
            device_id_type=MESH,
        )
        made.start()
        self.sent.append(made)
        return made

    def settle(self, made):
        made.wait_recv()
        made.wait_send()
        self.sent = [copy for copy in self.sent if copy is not made]

    def drain(self):
        for made in self.sent:
            made.wait_send()
        self.sent = []


def body(
    h1_hbm, h2_hbm, partner_ref, down_hbm, up_ref,
    loss_ref, g1_ref, g2_ref, gdown_ref, gup_ref,
    h, down, unit, inv, low, q, k, expo, rowacc, colacc, rows, cols, row_in, row_pair_in, row_sib_in, col_in, col_pair_in,
    w, colb, pq, pk, sib_out, sib_in, q_out, q_in, k_out, k_in, pos, gm, gl,
    gsum, core_in, x_out, x_in, y_out, y_in, z_all, y_all, x_all, core_all,
    loss_core, loss_x, loss_y, loss_z,
    load_sems, send_sems, recv_sems,
):
    blk, grp = lax.axis_index("blk"), lax.axis_index("grp")
    x, z_hi = lax.div(blk, 2), lax.rem(blk, 2)
    z_lo, y, core = lax.div(grp, 8), lax.rem(lax.div(grp, 2), 4), lax.rem(grp, 2)
    z = z_hi * 2 + z_lo

    def at(dx=0, dy=0, dz=0, other=False):
        px, py, pz = lax.rem(x + dx, 4), lax.rem(y + dy, 4), lax.rem(z + dz, 4)
        pc = 1 - core if other else core
        return (px * 2 + lax.div(pz, 2), lax.rem(pz, 2) * 8 + py * 2 + pc)

    odd = lax.rem(z, 2)
    sibling = at(other=True)
    q_pair = at(dz=1 + 2 * odd)
    k_pair = at(dz=3 - 2 * odd)
    q_ring = {step: at(dy=step) for step in (1, 2, 3)}
    k_ring = {step: at(dx=step) for step in (1, 2, 3)}
    z_ring = {step: at(dz=step) for step in (1, 2, 3)}
    links = Links(send_sems, recv_sems)

    loads = [
        pltpu.make_async_copy(h1_hbm, h.at[0:ROWS], load_sems.at[0]),
        pltpu.make_async_copy(h2_hbm, h.at[ROWS : 2 * ROWS], load_sems.at[1]),
        pltpu.make_async_copy(down_hbm, down, load_sems.at[2]),
    ]
    for load in loads:
        load.start()
    barrier = pltpu.get_barrier_semaphore()
    partners = [sibling, *q_ring.values(), *k_ring.values(), *z_ring.values()]
    for device in partners:
        pl.semaphore_signal(barrier, inc=1, device_id=device, device_id_type=MESH)
    rowacc[...] = jnp.zeros_like(rowacc)
    colacc[...] = jnp.zeros_like(colacc)
    for load in loads:
        load.wait()

    reduced = nt(h[...], down[...]).astype(BF16)
    low[...] = reduced
    mixed = h[:, 0:WIDTH].astype(F32) + nn(reduced, up_ref[...])
    inverse = lax.rsqrt(jnp.sum(mixed * mixed, axis=1, keepdims=True) + EPS)
    inv[...] = jnp.broadcast_to(inverse, inv.shape)
    normal = mixed * inverse
    unit[...] = normal
    q[0:ROWS, :] = normal[0:ROWS].astype(BF16)
    k[0:ROWS, :] = normal[ROWS:].astype(BF16)
    pl.semaphore_wait(barrier, len(partners))

    def q_at(slot, half=None):
        first = slot * 2 * ROWS
        return q.at[first : first + ROWS] if half is None else q.at[first + half * HALF : first + (half + 1) * HALF]

    def k_at(slot, half=None):
        first = slot * ROWS
        return k.at[first : first + ROWS] if half is None else k.at[first + half * HALF : first + (half + 1) * HALF]

    def to_sibling(slot):
        first = slot * 2 * ROWS
        return links.copy(q.at[first : first + ROWS], q.at[first + ROWS : first + 2 * ROWS], sibling)

    first_hop = []
    for at_slot, ring, pair in ((q_at, q_ring, q_pair), (k_at, k_ring, k_pair)):
        first_hop.append(
            (
                links.copy(at_slot(OWN), at_slot(DOWN), ring[1]),
                links.copy(at_slot(OWN), at_slot(UP), ring[3]),
                links.copy(at_slot(OWN), at_slot(PAIR), pair),
            )
        )
    passed = {OWN: to_sibling(OWN)}
    second_hop = []
    for (from_down, from_up, _), (at_slot, ring) in zip(first_hop, ((q_at, q_ring), (k_at, k_ring))):
        from_down.wait_recv()
        one = links.copy(at_slot(DOWN, 0), at_slot(FAR, 0), ring[1])
        from_up.wait_recv()
        two = links.copy(at_slot(UP, 1), at_slot(FAR, 1), ring[3])
        second_hop.append((one, two))
    for slot in (DOWN, UP):
        passed[slot] = to_sibling(slot)
    pair_hop = []
    for (_, _, from_pair), (at_slot, ring) in zip(first_hop, ((q_at, q_ring), (k_at, k_ring))):
        from_pair.wait_recv()
        pair_hop.append(
            (
                links.copy(at_slot(PAIR), at_slot(DOWN_PAIR), ring[1]),
                links.copy(at_slot(PAIR), at_slot(UP_PAIR), ring[3]),
            )
        )
    passed[PAIR] = to_sibling(PAIR)

    def score(first_row, row_count, first_col, col_count):
        def chunk(step, carry):
            here = pl.ds(pl.multiple_of(first_row + step * 256, 256), 256)
            columns = pl.ds(first_col, col_count)
            value = jnp.exp(SCALE * nt(q[here, :], k[columns, :]) - SCALE)
            expo[here, columns] = value
            colacc[:, columns] += jnp.sum(value.reshape(32, 8, col_count), axis=0)
            total = value[:, 0:LANES]
            for lane in range(LANES, col_count, LANES):
                total = total + value[:, lane : lane + LANES]
            rowacc[here, :] += total
            return carry

        lax.fori_loop(0, row_count // 256, chunk, 0)

    for slot in (OWN, UP, DOWN, PAIR):
        passed[slot].wait_recv()
    score(0, 1024, 0, 512)
    third_hop = []
    for halves, (at_slot, pair) in zip(second_hop, ((q_at, q_pair), (k_at, k_pair))):
        for half in halves:
            half.wait_recv()
        third_hop.append(links.copy(at_slot(FAR), at_slot(FAR_PAIR), pair))
    passed[FAR] = to_sibling(FAR)
    for from_down, from_up in pair_hop:
        from_down.wait_recv()
        from_up.wait_recv()
    for slot in (DOWN_PAIR, UP_PAIR):
        passed[slot] = to_sibling(slot)
    score(0, 1024, 512, 256)
    for slot in (FAR, DOWN_PAIR, UP_PAIR):
        passed[slot].wait_recv()
    score(1024, 768, 0, 768)
    for arrival in third_hop:
        arrival.wait_recv()
    passed[FAR_PAIR] = to_sibling(FAR_PAIR)
    score(0, 1792, 768, 256)
    passed[FAR_PAIR].wait_recv()
    score(1792, 256, 0, 1024)
    links.drain()

    for block in range(16):
        lanes = rowacc[block * ROWS : (block + 1) * ROWS, :].T
        rows[block : block + 1, :] = jnp.sum(lanes, axis=0, keepdims=True)
    for block in range(8):
        cols[block : block + 1, :] = jnp.sum(colacc[:, block * LANES : (block + 1) * LANES], axis=0, keepdims=True)
    row_swap = links.copy(rows, row_sib_in, sibling)
    col_swap = {step: links.copy(cols, col_in.at[step - 1], k_ring[step]) for step in (1, 2, 3)}
    links.settle(row_swap)
    for slot in range(8):
        for rank in range(2):
            here, there = slot * 2 + rank, slot * 2 + 1 - rank
            rows[here : here + 1, :] = rows[here : here + 1, :] + row_sib_in[there : there + 1, :]
    row_copies = {step: links.copy(rows, row_in.at[step - 1], q_ring[step]) for step in (1, 2, 3)}

    def ring_sum(total, arrived, copies, width):
        for copy in copies.values():
            links.settle(copy)
        sums = []
        for slot in range(8):
            along, half = PLACE[slot]
            value = total[slot * width : (slot + 1) * width, :]
            for step in (1, 2, 3):
                there = SLOT[((along + step) % 4, half)]
                value = value + arrived[step - 1, there * width : (there + 1) * width, :]
            sums.append(value)
        for slot in range(8):
            total[slot * width : (slot + 1) * width, :] = sums[slot]

    def pair_sum(total, arrived, copy, width):
        links.settle(copy)
        for slot in range(8):
            along, half = PLACE[slot]
            there = SLOT[(along, 1 - half)]
            here = slice(slot * width, (slot + 1) * width)
            total[here, :] = total[here, :] + arrived[there * width : (there + 1) * width, :]

    ring_sum(cols, col_in, col_swap, 1)
    col_pair = links.copy(cols, col_pair_in, k_pair)
    ring_sum(rows, row_in, row_copies, 2)
    row_pair = links.copy(rows, row_pair_in, q_pair)
    pair_sum(cols, col_pair_in, col_pair, 1)
    col_half = 0.5 / cols[...]
    for block in range(8):
        colb[0:1, block * LANES : (block + 1) * LANES] = col_half[block : block + 1, :]
    pair_sum(rows, row_pair_in, row_pair, 2)

    choice = (lax.broadcasted_iota(jnp.int32, (ROWS, ROWS), 0) == partner_ref[...]).astype(BF16)
    pos[0:ROWS, :] = tn(choice, k[0:ROWS, :])
    pos[ROWS : 2 * ROWS, :] = nn(choice, q[0:ROWS, :])
    positive = SCALE * jnp.sum(q[0:ROWS, :].astype(F32) * pos[0:ROWS, :])
    terms = 0.5 * jnp.sum(jnp.log(rows[0:1, :])) + 0.5 * jnp.sum(jnp.log(cols[0:1, :])) - positive
    loss_core[core, :, :] = jnp.broadcast_to(terms, (8, LANES))
    loss_swap = [links.copy(loss_core.at[core], loss_core.at[core], sibling)]

    def loss_step(copies, before, after, place, ring):
        for copy in copies:
            copy.wait_recv()
        after[place, :, :] = jnp.sum(before[...], axis=0)
        return [links.copy(after.at[place], after.at[place], ring[step]) for step in (1, 2, 3)]

    row_half = 0.5 / rows[...]
    for block in range(16):
        rows[block : block + 1, :] = row_half[block : block + 1, :]

    def weigh(block, carry):
        here = pl.ds(pl.multiple_of(block * ROWS, ROWS), ROWS)
        row = jnp.broadcast_to(rows[pl.ds(block, 1), :], (ROWS, ROWS)).T
        for lane in range(0, WIDTH, LANES):
            columns = slice(lane, lane + LANES)
            w[here, columns] = (expo[here, columns] * (row + colb[0:1, columns])).astype(BF16)
        return carry

    lax.fori_loop(0, 16, weigh, 0)

    def key_part(first):
        pk[first : first + 256, :] = tn(w[:, first : first + 256], q[...])

    def query_part(slot):
        here = slot * 2 * ROWS
        part = nn(w[here : here + 2 * ROWS, :], k[...])
        pq[slot, :, :] = part[0:ROWS]
        sib_out[slot, :, :] = part[ROWS:].astype(BF16)
        return links.copy(sib_out.at[slot], sib_in.at[slot], sibling)

    def k_part(slot):
        return pk[slot * ROWS : (slot + 1) * ROWS, :]

    def q_part(slot):
        sib[slot].wait_recv()
        return pq[slot] + sib_in[slot].astype(F32)

    def send(value, out, landing, index, device):
        out[index, :, :] = value.astype(BF16)
        return links.copy(out.at[index], landing.at[index], device)

    k_got, q_got, sib = {}, {}, {}
    key_part(768)
    k_got[0] = send(k_part(FAR_PAIR), k_out, k_in, 0, k_pair)
    k_got[2] = send(k_part(DOWN_PAIR), k_out, k_in, 2, k_ring[3])
    for slot in (FAR_PAIR, DOWN_PAIR, UP_PAIR):
        sib[slot] = query_part(slot)
    key_part(512)
    k_got[1] = send(k_part(UP_PAIR), k_out, k_in, 1, k_ring[1])
    q_got[0] = send(q_part(FAR_PAIR), q_out, q_in, 0, q_pair)
    q_got[2] = send(q_part(DOWN_PAIR), q_out, q_in, 2, q_ring[3])
    q_got[1] = send(q_part(UP_PAIR), q_out, q_in, 1, q_ring[1])
    loss_copies = loss_step(loss_swap, loss_core, loss_x, x, k_ring)
    for slot in (FAR, PAIR, DOWN, UP, OWN):
        sib[slot] = query_part(slot)
    loss_copies = loss_step(loss_copies, loss_x, loss_y, y, q_ring)
    key_part(256)
    key_part(0)
    loss_copies = loss_step(loss_copies, loss_y, loss_z, z, z_ring)

    def far_halves(part, got, out, landing, ring):
        got[0].wait_recv()
        value = (part(FAR) + landing[0].astype(F32)).astype(BF16)
        out[3, :, :] = value
        return (
            links.copy(out.at[3, 0:HALF], landing.at[3, 0:HALF], ring[3]),
            links.copy(out.at[3, HALF:ROWS], landing.at[3, HALF:ROWS], ring[1]),
        )

    k_far = far_halves(k_part, k_got, k_out, k_in, k_ring)
    q_far = far_halves(q_part, q_got, q_out, q_in, q_ring)

    def pair_back(part, got, out, landing, pair):
        got[1].wait_recv()
        got[2].wait_recv()
        value = part(PAIR) + landing[1].astype(F32) + landing[2].astype(F32)
        got[6] = send(value, out, landing, 6, pair)

    pair_back(k_part, k_got, k_out, k_in, k_pair)
    pair_back(q_part, q_got, q_out, q_in, q_pair)

    def ring_back(part, got, far, out, landing, ring):
        far[0].wait_recv()
        value = part(DOWN)
        out[5, :, :] = jnp.concatenate([value[0:HALF] + landing[3, 0:HALF].astype(F32), value[HALF:]], axis=0).astype(BF16)
        got[5] = links.copy(out.at[5], landing.at[5], ring[3])
        far[1].wait_recv()
        value = part(UP)
        out[4, :, :] = jnp.concatenate([value[0:HALF], value[HALF:] + landing[3, HALF:ROWS].astype(F32)], axis=0).astype(BF16)
        got[4] = links.copy(out.at[4], landing.at[4], ring[1])

    ring_back(k_part, k_got, k_far, k_out, k_in, k_ring)
    ring_back(q_part, q_got, q_far, q_out, q_in, q_ring)
    for copy in loss_copies:
        copy.wait_recv()
    loss_ref[...] = jnp.sum(loss_z[...], axis=0) * (1.0 / TEXTS) + SCALE

    for view, (part, got, landing) in enumerate(((k_part, k_got, k_in), (q_part, q_got, q_in))):
        first = ROWS * (1 - view)
        here = slice(first, first + ROWS)
        for index in (4, 5, 6):
            got[index].wait_recv()
        total = part(OWN) + landing[4].astype(F32) + landing[5].astype(F32) + landing[6].astype(F32)
        gradient = SCALE * (total - pos[here, :])
        normal = unit[here, :]
        along = jnp.sum(normal * gradient, axis=1, keepdims=True)
        gm[here, :] = (inv[here, 0:1] * (gradient - normal * along)).astype(BF16)
    gl[...] = nt(gm[...], up_ref[...]).astype(BF16)
    low_rows = gl[...].astype(F32).T.astype(BF16)

    def down_chunk(step, carry):
        columns = pl.ds(pl.multiple_of(step * 512, 512), 512)
        gsum[:, columns] = nn(low_rows, h[:, columns])
        return carry

    lax.fori_loop(0, MODEL // 512, down_chunk, 0)
    gsum[:, MODEL : MODEL + WIDTH] = tn(low[...], gm[...])

    half_rows = RANK // 2
    quarter = (MODEL + WIDTH) // 4
    eighth = quarter // 2
    mine = pl.ds(pl.multiple_of(core * half_rows, half_rows), half_rows)
    theirs = pl.ds(pl.multiple_of((1 - core) * half_rows, half_rows), half_rows)
    core_all[...] = gsum[theirs, :].astype(BF16)
    core_got = links.copy(core_all, core_in, sibling)

    def state(first, out_ref, first_col, col_count, with_mixed):
        here = slice(first, first + ROWS)

        def chunk(step, carry):
            columns = pl.ds(pl.multiple_of(first_col + step * 512, 512), 512)
            value = nn(gl[here, :], down[:, columns])
            if with_mixed:
                value = value + gm[here, columns].astype(F32)
            out_ref[:, columns] = value.astype(BF16)
            return carry

        lax.fori_loop(0, col_count // 512, chunk, 0)

    core_got.wait_recv()
    for place in range(4):
        columns = slice(place * quarter, (place + 1) * quarter)
        value = gsum[mine, columns] + core_in[:, columns].astype(F32)
        gsum[mine, columns] = value
        x_out[place, :, :] = value.astype(BF16)
    x_got = {step: links.copy(x_out.at[lax.rem(x + step, 4)], x_in.at[step - 1], k_ring[step]) for step in (1, 2, 3)}
    state(0, g1_ref, 0, WIDTH, True)
    state(0, g1_ref, WIDTH, MODEL - WIDTH, False)
    for copy in x_got.values():
        copy.wait_recv()
    value = x_out[x].astype(F32) + x_in[0].astype(F32) + x_in[1].astype(F32) + x_in[2].astype(F32)
    for place in range(4):
        top, side = (place // 2) * 16, (place % 2) * eighth
        y_out[place, :, :] = value[top : top + 16, side : side + eighth].astype(BF16)
    y_got = {step: links.copy(y_out.at[lax.rem(y + step, 4)], y_in.at[step - 1], q_ring[step]) for step in (1, 2, 3)}
    state(ROWS, g2_ref, 0, WIDTH, True)
    for copy in y_got.values():
        copy.wait_recv()
    value = y_out[y].astype(F32) + y_in[0].astype(F32) + y_in[1].astype(F32) + y_in[2].astype(F32)
    z_all[z, :, :] = value.astype(BF16)
    z_got = [links.copy(z_all.at[z], z_all.at[z], z_ring[step]) for step in (1, 2, 3)]
    state(ROWS, g2_ref, WIDTH, MODEL - WIDTH, False)
    for copy in z_got:
        copy.wait_recv()
    y_all[y, :, :] = jnp.sum(z_all[...].astype(F32), axis=0).astype(BF16)
    y_back = [links.copy(y_all.at[y], y_all.at[y], q_ring[step]) for step in (1, 2, 3)]
    for copy in y_back:
        copy.wait_recv()
    for place in range(4):
        top, side = (place // 2) * 16, (place % 2) * eighth
        x_all[core, x, top : top + 16, side : side + eighth] = y_all[place]
    x_back = [links.copy(x_all.at[core, x], x_all.at[core, x], k_ring[step]) for step in (1, 2, 3)]
    core_sends = [links.copy(x_all.at[core, x], x_all.at[core, x], sibling)]
    for copy in x_back:
        copy.wait_recv()
    for step in (1, 2, 3):
        came = lax.rem(x + 4 - step, 4)
        core_sends.append(links.copy(x_all.at[core, came], x_all.at[core, came], sibling))
    for copy in core_sends:
        copy.wait_recv()
    for rank in range(2):
        top = slice(rank * half_rows, (rank + 1) * half_rows)
        for place in range(4):
            value = x_all[rank, place].astype(F32)
            first = place * quarter
            last = first + quarter
            if last <= MODEL:
                gdown_ref[top, first:last] = value
            else:
                gdown_ref[top, first:MODEL] = value[:, 0 : MODEL - first]
                gup_ref[top, :] = value[:, MODEL - first :]
    links.drain()


def shards(first_pooled_view, second_pooled_view, partner, adapter_down_weight, adapter_up_weight):
    vmem, hbm = pl.BlockSpec(memory_space=pltpu.VMEM), pl.BlockSpec(memory_space=pl.ANY)
    total = MODEL + WIDTH
    quarter = total // 4
    loss, first_gradient, second_gradient, down_rows, grad_up = pl.pallas_call(
        body,
        out_shape=(
            jax.ShapeDtypeStruct((8, LANES), F32),
            jax.ShapeDtypeStruct((ROWS, MODEL), BF16),
            jax.ShapeDtypeStruct((ROWS, MODEL), BF16),
            jax.ShapeDtypeStruct((RANK, MODEL), F32),
            jax.ShapeDtypeStruct((RANK, WIDTH), F32),
        ),
        in_specs=[hbm, hbm, vmem, hbm, vmem],
        out_specs=(vmem, vmem, vmem, vmem, vmem),
        scratch_shapes=[
            pltpu.VMEM((2 * ROWS, MODEL), BF16),
            pltpu.VMEM((RANK, MODEL), BF16),
            pltpu.VMEM((2 * ROWS, WIDTH), F32),
            pltpu.VMEM((2 * ROWS, LANES), F32),
            pltpu.VMEM((2 * ROWS, RANK), BF16),
            pltpu.VMEM((16 * ROWS, WIDTH), BF16),
            pltpu.VMEM((8 * ROWS, WIDTH), BF16),
            pltpu.VMEM((16 * ROWS, 8 * ROWS), F32),
            pltpu.VMEM((16 * ROWS, LANES), F32),
            pltpu.VMEM((8, 8 * ROWS), F32),
            pltpu.VMEM((16, LANES), F32),
            pltpu.VMEM((8, LANES), F32),
            pltpu.VMEM((3, 16, LANES), F32),
            pltpu.VMEM((16, LANES), F32),
            pltpu.VMEM((16, LANES), F32),
            pltpu.VMEM((3, 8, LANES), F32),
            pltpu.VMEM((8, LANES), F32),
            pltpu.VMEM((16 * ROWS, 8 * ROWS), BF16),
            pltpu.VMEM((8, 8 * ROWS), F32),
            pltpu.VMEM((8, ROWS, WIDTH), F32),
            pltpu.VMEM((8 * ROWS, WIDTH), F32),
            pltpu.VMEM((8, ROWS, WIDTH), BF16),
            pltpu.VMEM((8, ROWS, WIDTH), BF16),
            pltpu.VMEM((7, ROWS, WIDTH), BF16),
            pltpu.VMEM((7, ROWS, WIDTH), BF16),
            pltpu.VMEM((7, ROWS, WIDTH), BF16),
            pltpu.VMEM((7, ROWS, WIDTH), BF16),
            pltpu.VMEM((2 * ROWS, WIDTH), F32),
            pltpu.VMEM((2 * ROWS, WIDTH), BF16),
            pltpu.VMEM((2 * ROWS, RANK), BF16),
            pltpu.VMEM((RANK, total), F32),
            pltpu.VMEM((RANK // 2, total), BF16),
            pltpu.VMEM((4, RANK // 2, quarter), BF16),
            pltpu.VMEM((3, RANK // 2, quarter), BF16),
            pltpu.VMEM((4, 16, quarter // 2), BF16),
            pltpu.VMEM((3, 16, quarter // 2), BF16),
            pltpu.VMEM((4, 16, quarter // 2), BF16),
            pltpu.VMEM((4, 16, quarter // 2), BF16),
            pltpu.VMEM((2, 4, RANK // 2, quarter), BF16),
            pltpu.VMEM((RANK // 2, total), BF16),
            pltpu.VMEM((2, 8, LANES), F32),
            pltpu.VMEM((4, 8, LANES), F32),
            pltpu.VMEM((4, 8, LANES), F32),
            pltpu.VMEM((4, 8, LANES), F32),
            pltpu.SemaphoreType.DMA((3,)),
            pltpu.SemaphoreType.DMA((COPIES,)),
            pltpu.SemaphoreType.DMA((COPIES,)),
        ],
        compiler_params=pltpu.CompilerParams(
            collective_id=0, has_side_effects=True, vmem_limit_bytes=60 * 1024 * 1024
        ),
    )(first_pooled_view, second_pooled_view, partner, adapter_down_weight.T, adapter_up_weight)
    return (loss[0, 0], first_gradient, second_gradient, down_rows.T, grad_up)


def solution(mesh):
    in_specs = (P(("blk", "grp"), None), P(("blk", "grp"), None), P(("blk", "grp"), None), P(), P())
    out_specs = (P(), P(("blk", "grp"), None), P(("blk", "grp"), None), P(), P())
    return jax.shard_map(shards, mesh=mesh, in_specs=in_specs, out_specs=out_specs, check_vma=False)
```

```python
import jax
import jax.numpy as jnp
from jax import lax
from jax.experimental import pallas as pl
from jax.experimental.pallas import tpu as pltpu
from jax.sharding import PartitionSpec as P

SCALE = 20.0
EPS = 1e-06
MESH = pl.DeviceIdType.MESH
F32 = jnp.float32
BF16 = jnp.bfloat16

ROWS = 128
WIDTH = 1024
MODEL = 4096
RANK = 64
LANES = 128
TEXTS = 16384

ORDER = (0, 1, 2, 4, 3, 6, 5, 7)
SLOT = {mask: slot for slot, mask in enumerate(ORDER)}
BACK = {(7, 0): 1, (7, 1): 4}
BACK.update({(mask, half): link for mask, link in ((6, 2), (3, 1), (5, 4), (1, 1), (2, 2), (4, 4)) for half in (0, 1)})
HALF = ROWS // 2
COPIES = 176
TOTAL = MODEL + WIDTH
HALF_RANK = RANK // 2
PIECE = TOTAL // 8


def nn(a, b):
    return lax.dot_general(a, b, (((1,), (0,)), ((), ())), preferred_element_type=F32)


def nt(a, b):
    return lax.dot_general(a, b, (((1,), (1,)), ((), ())), preferred_element_type=F32)


def tn(a, b):
    return lax.dot_general(a, b, (((0,), (0,)), ((), ())), preferred_element_type=F32)


class Links:
    def __init__(self, send_sems, recv_sems):
        self.send_sems, self.recv_sems, self.count, self.sent = send_sems, recv_sems, 0, []

    def copy(self, src, dst, device):
        index = self.count
        self.count += 1
        made = pltpu.make_async_remote_copy(
            src_ref=src,
            dst_ref=dst,
            send_sem=self.send_sems.at[index],
            recv_sem=self.recv_sems.at[index],
            device_id=device,
            device_id_type=MESH,
        )
        made.start()
        self.sent.append(made)
        return made

    def settle(self, made):
        made.wait_recv()
        made.wait_send()
        self.sent = [copy for copy in self.sent if copy is not made]

    def drain(self):
        for made in self.sent:
            made.wait_send()
        self.sent = []


def half_rows(half):
    return slice(half * HALF, (half + 1) * HALF)


class Group:
    def __init__(self, links, near, data, stride, out, landing, part):
        self.links, self.near, self.data, self.stride = links, near, data, stride
        self.out, self.landing, self.part, self.got, self.back_got = out, landing, part, {}, {}

    def at(self, mask, half):
        first = SLOT[mask] * self.stride + half * HALF
        return self.data.at[first : first + HALF]

    def give(self, mask, half, link):
        there = mask ^ link
        self.got[there, half] = self.links.copy(self.at(mask, half), self.at(there, half), self.near[link])

    def have(self, mask, half):
        self.got[mask, half].wait_recv()

    def back(self, mask, half, add=None):
        rows = half_rows(half)
        value = self.part(mask, rows)
        if add is not None:
            self.back_got[add, half].wait_recv()
            value = value + self.landing[add - 1, rows].astype(F32)
        self.out[mask - 1, rows] = value.astype(BF16)
        self.back_got[mask, half] = self.links.copy(
            self.out.at[mask - 1, rows], self.landing.at[mask - 1, rows], self.near[BACK[mask, half]]
        )

    def whole(self):
        total = self.part(0, slice(0, ROWS))
        for mask in (1, 2, 4):
            for half in (0, 1):
                self.back_got[mask, half].wait_recv()
        for mask in (1, 2, 4):
            total = total + self.landing[mask - 1].astype(F32)
        return total


def body(
    h1_hbm, h2_hbm, partner_ref, down_hbm, up_ref,
    loss_ref, gl, gm, sums,
    h, down, unit, inv, low, q, k, expo, rowacc, colacc, rows, cols, row_in, row_sib_in, col_in,
    w, colb, pq, pk, sib_out, sib_in, q_out, q_in, k_out, k_in, pos,
    gsum, gsend, core_in, plane_out, plane_in, z_all,
    loss_core, loss_plane, loss_z,
    load_sems, send_sems, recv_sems,
):
    blk, grp = lax.axis_index("blk"), lax.axis_index("grp")
    x, z_hi = lax.div(blk, 2), lax.rem(blk, 2)
    z_lo, y, core = lax.div(grp, 8), lax.rem(lax.div(grp, 2), 4), lax.rem(grp, 2)
    z = z_hi * 2 + z_lo
    place = x * 4 + y

    def at(dx=0, dy=0, dz=0, other=False):
        px, py, pz = lax.rem(x + dx, 4), lax.rem(y + dy, 4), lax.rem(z + dz, 4)
        pc = 1 - core if other else core
        return (px * 2 + lax.div(pz, 2), lax.rem(pz, 2) * 8 + py * 2 + pc)

    up_or_down = [1 + 2 * lax.rem(c, 2) for c in (x, y, z)]

    def cube(flip):
        steps = [4 - s if flip else s for s in up_or_down]
        return {m: at(*(s if m & bit else 0 for bit, s in zip((1, 2, 4), steps))) for m in range(1, 8)}

    sibling = at(other=True)
    q_near, k_near = cube(False), cube(True)
    plane = {(dx, dy): at(dx, dy) for dx in range(4) for dy in range(4) if dx or dy}
    column = {dz: at(dz=dz) for dz in (1, 2, 3)}
    links = Links(send_sems, recv_sems)

    loads = [
        pltpu.make_async_copy(h1_hbm, h.at[0:ROWS], load_sems.at[0]),
        pltpu.make_async_copy(h2_hbm, h.at[ROWS : 2 * ROWS], load_sems.at[1]),
        pltpu.make_async_copy(down_hbm, down, load_sems.at[2]),
    ]
    for load in loads:
        load.start()
    partners = [sibling, *plane.values(), *column.values()]
    partners += [near[m] for near in (q_near, k_near) for m in (5, 6, 7)]
    barrier = pltpu.get_barrier_semaphore()
    for device in partners:
        pl.semaphore_signal(barrier, inc=1, device_id=device, device_id_type=MESH)
    rowacc[...] = jnp.zeros_like(rowacc)
    colacc[...] = jnp.zeros_like(colacc)
    for load in loads:
        load.wait()

    low[...] = nt(h[...], down[...]).astype(BF16)
    for view, own in enumerate((q, k)):
        here = slice(view * ROWS, (view + 1) * ROWS)
        mixed = h[here, 0:WIDTH].astype(F32) + nn(low[here, :], up_ref[...])
        inverse = lax.rsqrt(jnp.sum(mixed * mixed, axis=1, keepdims=True) + EPS)
        inv[here, :] = jnp.broadcast_to(inverse, (ROWS, LANES))
        normal = mixed * inverse
        unit[here, :] = normal
        own[0:ROWS, :] = normal.astype(BF16)
    pl.semaphore_wait(barrier, len(partners))

    sib = {}

    def q_part(mask, here):
        return pq[SLOT[mask], here, :] + sib_in[SLOT[mask], here, :].astype(F32)

    def k_part(mask, here):
        first = SLOT[mask] * ROWS
        return pk[first + here.start : first + here.stop, :]

    queries = Group(links, q_near, q, 2 * ROWS, q_out, q_in, q_part)
    keys = Group(links, k_near, k, ROWS, k_out, k_in, k_part)
    groups = (queries, keys)

    def to_sibling(mask):
        first = SLOT[mask] * 2 * ROWS
        return links.copy(q.at[first : first + ROWS], q.at[first + ROWS : first + 2 * ROWS], sibling)

    FIRST = {1: 0, 2: 1, 4: 0}
    NEXT = {4: 2, 2: 1, 1: 4}
    for turn in (0, 1):
        for group in groups:
            for link in (1, 2, 4):
                group.give(0, FIRST[link] ^ turn, link)
    passed = {0: to_sibling(0)}
    for turn in (0, 1):
        for group in groups:
            for mask in (4, 2, 1):
                group.have(mask, FIRST[mask] ^ turn)
                group.give(mask, FIRST[mask] ^ turn, NEXT[mask])
    for mask in (1, 2, 4):
        passed[mask] = to_sibling(mask)

    def score(first_row, row_count, first_col, col_count):
        def chunk(step, carry):
            here = pl.ds(pl.multiple_of(first_row + step * 256, 256), 256)
            columns = pl.ds(first_col, col_count)
            value = jnp.exp(SCALE * nt(q[here, :], k[columns, :]) - SCALE)
            expo[here, columns] = value
            colacc[:, columns] += jnp.sum(value.reshape(32, 8, col_count), axis=0)
            total = value[:, 0:LANES]
            for lane in range(LANES, col_count, LANES):
                total = total + value[:, lane : lane + LANES]
            rowacc[here, :] += total
            return carry

        lax.fori_loop(0, row_count // 256, chunk, 0)

    for mask in (0, 1, 2, 4):
        passed[mask].wait_recv()
    score(0, 1024, 0, 512)
    for group in groups:
        group.have(6, 0)
        group.give(6, 0, 1)
        group.have(3, 1)
        group.give(3, 1, 4)
    for mask, half in ((6, 1), (3, 0), (5, 0), (5, 1)):
        for group in groups:
            group.have(mask, half)
    for mask in (3, 6, 5):
        passed[mask] = to_sibling(mask)
    score(0, 1024, 512, 256)
    for mask in (3, 6, 5):
        passed[mask].wait_recv()
    score(1024, 768, 0, 768)
    for half in (0, 1):
        queries.have(7, half)
    passed[7] = to_sibling(7)
    for half in (0, 1):
        keys.have(7, half)
    score(0, 1792, 768, 256)
    passed[7].wait_recv()
    score(1792, 256, 0, 1024)
    links.drain()

    for block in range(8):
        cols[block : block + 1, :] = jnp.sum(colacc[:, block * LANES : (block + 1) * LANES], axis=0, keepdims=True)
    col_copies = {m: links.copy(cols, col_in.at[m - 1], k_near[m]) for m in range(1, 8)}
    for block in range(16):
        lanes = rowacc[block * ROWS : (block + 1) * ROWS, :].T
        rows[block : block + 1, :] = jnp.sum(lanes, axis=0, keepdims=True)
    row_swap = links.copy(rows, row_sib_in, sibling)
    links.settle(row_swap)
    for slot in range(8):
        for rank in range(2):
            here, there = slot * 2 + rank, slot * 2 + 1 - rank
            rows[here : here + 1, :] = rows[here : here + 1, :] + row_sib_in[there : there + 1, :]
    row_copies = {m: links.copy(rows, row_in.at[m - 1], q_near[m]) for m in range(1, 8)}

    choice = (lax.broadcasted_iota(jnp.int32, (ROWS, ROWS), 0) == partner_ref[...]).astype(BF16)
    pos[0:ROWS, :] = tn(choice, k[0:ROWS, :])
    pos[ROWS : 2 * ROWS, :] = nn(choice, q[0:ROWS, :])
    positive = SCALE * jnp.sum(q[0:ROWS, :].astype(F32) * pos[0:ROWS, :])

    def cube_sum(total, arrived, copies, width):
        for copy in copies.values():
            links.settle(copy)
        sums = []
        for mask in ORDER:
            value = total[SLOT[mask] * width : (SLOT[mask] + 1) * width, :]
            for m in range(1, 8):
                there = SLOT[mask ^ m] * width
                value = value + arrived[m - 1, there : there + width, :]
            sums.append(value)
        return sums

    sums_of_cols = cube_sum(cols, col_in, col_copies, 1)
    for slot, value in enumerate(sums_of_cols):
        colb[0:1, slot * LANES : (slot + 1) * LANES] = 0.5 / value
    sums_of_rows = cube_sum(rows, row_in, row_copies, 2)
    for slot, value in enumerate(sums_of_rows):
        rows[2 * slot : 2 * slot + 2, :] = 0.5 / value

    def weigh(block, carry):
        here = pl.ds(pl.multiple_of(block * ROWS, ROWS), ROWS)
        row = jnp.broadcast_to(rows[pl.ds(block, 1), :], (ROWS, ROWS)).T
        for lane in range(0, WIDTH, LANES):
            columns = slice(lane, lane + LANES)
            w[here, columns] = (expo[here, columns] * (row + colb[0:1, columns])).astype(BF16)
        return carry

    lax.fori_loop(0, 16, weigh, 0)

    def key_part(first):
        pk[first : first + 256, :] = tn(w[:, first : first + 256], q[...])

    def query_part(mask):
        slot = SLOT[mask]
        here = slot * 2 * ROWS
        part = nn(w[here : here + 2 * ROWS, :], k[...])
        pq[slot, :, :] = part[0:ROWS]
        sib_out[slot, :, :] = part[ROWS:].astype(BF16)
        sib[mask] = links.copy(sib_out.at[slot], sib_in.at[slot], sibling)

    key_part(768)
    for mask, half in ((7, 0), (7, 1), (5, 0), (5, 1)):
        keys.back(mask, half)
    query_part(7)
    key_part(512)
    keys.back(3, 0)
    keys.back(6, 1)
    sib[7].wait_recv()
    queries.back(7, 0)
    queries.back(7, 1)
    for mask in (5, 3, 6):
        query_part(mask)
    sib[5].wait_recv()
    queries.back(5, 0)
    queries.back(5, 1)
    sib[3].wait_recv()
    queries.back(3, 0)
    sib[6].wait_recv()
    queries.back(6, 1)

    terms = 0.5 * jnp.sum(jnp.log(sums_of_rows[0][0:1, :])) + 0.5 * jnp.sum(jnp.log(sums_of_cols[0])) - positive
    loss_core[core, :, :] = jnp.broadcast_to(terms, (8, LANES))
    loss_swap = links.copy(loss_core.at[core], loss_core.at[core], sibling)
    key_part(256)
    keys.back(6, 0, 7)
    keys.back(3, 1, 7)
    for mask in (1, 2, 4):
        query_part(mask)
    loss_swap.wait_recv()
    loss_plane[place, :, :] = jnp.sum(loss_core[...], axis=0)
    loss_copies = [links.copy(loss_plane.at[place], loss_plane.at[place], device) for device in plane.values()]
    queries.back(6, 0, 7)
    queries.back(3, 1, 7)
    key_part(0)
    keys.back(1, 0, 5)
    keys.back(2, 0, 3)
    keys.back(4, 1, 6)
    keys.back(1, 1, 5)
    query_part(0)
    for mask in (1, 2, 4):
        sib[mask].wait_recv()
    queries.back(1, 0, 5)
    queries.back(2, 0, 3)
    queries.back(4, 1, 6)
    queries.back(1, 1, 5)
    keys.back(4, 0, 6)
    keys.back(2, 1, 3)
    queries.back(4, 0, 6)
    queries.back(2, 1, 3)
    sib[0].wait_recv()
    for copy in loss_copies:
        copy.wait_recv()
    loss_z[z, :, :] = jnp.sum(loss_plane[...], axis=0)
    loss_copies = [links.copy(loss_z.at[z], loss_z.at[z], device) for device in column.values()]

    for view, group in ((1, keys), (0, queries)):
        here = slice(view * ROWS, (view + 1) * ROWS)
        gradient = SCALE * (group.whole() - pos[here, :])
        normal = unit[here, :]
        along = jnp.sum(normal * gradient, axis=1, keepdims=True)
        gm[here, :] = (inv[here, 0:1] * (gradient - normal * along)).astype(BF16)
        small = nt(gm[here, :], up_ref[...])
        gl[here, :] = small.astype(BF16)
        small_rows = small.T.astype(BF16)

        def down_chunk(step, carry, here=here, small_rows=small_rows, view=view):
            columns = pl.ds(pl.multiple_of(step * 512, 512), 512)
            value = nn(small_rows, h[here, columns])
            if view == 0:
                value = value + gsum[:, columns]
                gsend[:, columns] = value.astype(BF16)
            gsum[:, columns] = value
            return carry

        lax.fori_loop(0, MODEL // 512, down_chunk, 0)
        value = tn(low[here, :], gm[here, :])
        if view == 0:
            value = value + gsum[:, MODEL:TOTAL]
            gsend[:, MODEL:TOTAL] = value.astype(BF16)
        gsum[:, MODEL:TOTAL] = value

    mine = pl.ds(pl.multiple_of(core * HALF_RANK, HALF_RANK), HALF_RANK)
    theirs = pl.ds(pl.multiple_of((1 - core) * HALF_RANK, HALF_RANK), HALF_RANK)
    core_got = links.copy(gsend.at[theirs], core_in, sibling)
    for copy in loss_copies:
        copy.wait_recv()
    loss_ref[0, 0] = jnp.sum(jnp.sum(loss_z[...], axis=0)[0:1, 0:1]) * (1.0 / TEXTS) + SCALE
    core_got.wait_recv()
    for piece in range(16):
        top, side = (piece // 8) * 16, (piece % 8) * PIECE
        columns = slice(side, side + PIECE)
        value = gsum[pl.ds(pl.multiple_of(core * HALF_RANK + top, 16), 16), columns]
        value = value + core_in[top : top + 16, columns].astype(F32)
        plane_out[piece, :, :] = value.astype(BF16)
    plane_got = []
    for (dx, dy), device in plane.items():
        there = lax.rem(x + dx, 4) * 4 + lax.rem(y + dy, 4)
        plane_got.append(links.copy(plane_out.at[there], plane_in.at[place], device))
    plane_in[place, :, :] = plane_out[place]
    for copy in plane_got:
        copy.wait_recv()
    z_all[z, :, :] = jnp.sum(plane_in[...].astype(F32), axis=0).astype(BF16)
    z_got = [links.copy(z_all.at[z], z_all.at[z], device) for device in column.values()]
    for copy in z_got:
        copy.wait_recv()
    sums[core, place, :, :] = jnp.sum(z_all[...].astype(F32), axis=0).astype(BF16)
    plane_back = {step: links.copy(sums.at[core, place], sums.at[core, place], device) for step, device in plane.items()}
    core_back = [links.copy(sums.at[core, place], sums.at[core, place], sibling)]
    for (dx, dy), copy in plane_back.items():
        copy.wait_recv()
        came = lax.rem(x + 4 - dx, 4) * 4 + lax.rem(y + 4 - dy, 4)
        core_back.append(links.copy(sums.at[core, came], sums.at[core, came], sibling))
    for copy in core_back:
        copy.wait_recv()
    links.drain()


def finish(
    loss_in, gl, gm, sums, down, loss_out, g1_hbm, g2_hbm, gdown_hbm, gup_hbm, state, grad_down, grad_up, sems
):
    loss_out[0, 0] = loss_in[0, 0]
    copies = []
    for view, target in enumerate((g1_hbm, g2_hbm)):
        here = slice(view * ROWS, (view + 1) * ROWS)
        value = nn(gl[here, :], down[:, 0:WIDTH]) + gm[here, :].astype(F32)
        state[view, :, 0:WIDTH] = value.astype(BF16)

        def chunk(step, carry, here=here, view=view):
            columns = pl.ds(pl.multiple_of(WIDTH + step * 1024, 1024), 1024)
            state[view, :, columns] = nn(gl[here, :], down[:, columns]).astype(BF16)
            return carry

        lax.fori_loop(0, MODEL // WIDTH - 1, chunk, 0)
        copies.append(pltpu.make_async_copy(state.at[view], target, sems.at[view]))
        copies[-1].start()
    for rank in range(2):
        for piece in range(16):
            top, first = rank * HALF_RANK + (piece // 8) * 16, (piece % 8) * PIECE
            last = first + PIECE
            value = sums[rank, piece].astype(F32)
            rows = slice(top, top + 16)
            if last <= MODEL:
                grad_down[rows, first:last] = value
            elif first < MODEL:
                grad_down[rows, first:MODEL] = value[:, 0 : MODEL - first]
                grad_up[rows, 0 : last - MODEL] = value[:, MODEL - first :]
            else:
                grad_up[rows, first - MODEL : last - MODEL] = value
    for source, target, index in ((grad_down, gdown_hbm, 2), (grad_up, gup_hbm, 3)):
        copies.append(pltpu.make_async_copy(source, target, sems.at[index]))
        copies[-1].start()
    for copy in copies:
        copy.wait()


def shards(first_pooled_view, second_pooled_view, partner, adapter_down_weight, adapter_up_weight):
    vmem, hbm = pl.BlockSpec(memory_space=pltpu.VMEM), pl.BlockSpec(memory_space=pl.ANY)
    smem = pl.BlockSpec(memory_space=pltpu.SMEM)
    down_rows = adapter_down_weight.T
    loss, small, mixed, sums = pl.pallas_call(
        body,
        out_shape=(
            jax.ShapeDtypeStruct((1, 1), F32),
            jax.ShapeDtypeStruct((2 * ROWS, RANK), BF16),
            jax.ShapeDtypeStruct((2 * ROWS, WIDTH), BF16),
            jax.ShapeDtypeStruct((2, 16, 16, PIECE), BF16),
        ),
        in_specs=[hbm, hbm, vmem, hbm, vmem],
        out_specs=(smem, vmem, vmem, vmem),
        scratch_shapes=[
            pltpu.VMEM((2 * ROWS, MODEL), BF16),
            pltpu.VMEM((RANK, MODEL), BF16),
            pltpu.VMEM((2 * ROWS, WIDTH), F32),
            pltpu.VMEM((2 * ROWS, LANES), F32),
            pltpu.VMEM((2 * ROWS, RANK), BF16),
            pltpu.VMEM((16 * ROWS, WIDTH), BF16),
            pltpu.VMEM((8 * ROWS, WIDTH), BF16),
            pltpu.VMEM((16 * ROWS, 8 * ROWS), F32),
            pltpu.VMEM((16 * ROWS, LANES), F32),
            pltpu.VMEM((8, 8 * ROWS), F32),
            pltpu.VMEM((16, LANES), F32),
            pltpu.VMEM((8, LANES), F32),
            pltpu.VMEM((7, 16, LANES), F32),
            pltpu.VMEM((16, LANES), F32),
            pltpu.VMEM((7, 8, LANES), F32),
            pltpu.VMEM((16 * ROWS, 8 * ROWS), BF16),
            pltpu.VMEM((8, 8 * ROWS), F32),
            pltpu.VMEM((8, ROWS, WIDTH), F32),
            pltpu.VMEM((8 * ROWS, WIDTH), F32),
            pltpu.VMEM((8, ROWS, WIDTH), BF16),
            pltpu.VMEM((8, ROWS, WIDTH), BF16),
            pltpu.VMEM((7, ROWS, WIDTH), BF16),
            pltpu.VMEM((7, ROWS, WIDTH), BF16),
            pltpu.VMEM((7, ROWS, WIDTH), BF16),
            pltpu.VMEM((7, ROWS, WIDTH), BF16),
            pltpu.VMEM((2 * ROWS, WIDTH), F32),
            pltpu.VMEM((RANK, TOTAL), F32),
            pltpu.VMEM((RANK, TOTAL), BF16),
            pltpu.VMEM((HALF_RANK, TOTAL), BF16),
            pltpu.VMEM((16, 16, PIECE), BF16),
            pltpu.VMEM((16, 16, PIECE), BF16),
            pltpu.VMEM((4, 16, PIECE), BF16),
            pltpu.VMEM((2, 8, LANES), F32),
            pltpu.VMEM((16, 8, LANES), F32),
            pltpu.VMEM((4, 8, LANES), F32),
            pltpu.SemaphoreType.DMA((3,)),
            pltpu.SemaphoreType.DMA((COPIES,)),
            pltpu.SemaphoreType.DMA((COPIES,)),
        ],
        compiler_params=pltpu.CompilerParams(
            collective_id=0, has_side_effects=True, vmem_limit_bytes=60 * 1024 * 1024
        ),
    )(first_pooled_view, second_pooled_view, partner, down_rows, adapter_up_weight)
    loss, first_gradient, second_gradient, grad_down, grad_up = pl.pallas_call(
        finish,
        out_shape=(
            jax.ShapeDtypeStruct((1, 1), F32),
            jax.ShapeDtypeStruct((ROWS, MODEL), BF16),
            jax.ShapeDtypeStruct((ROWS, MODEL), BF16),
            jax.ShapeDtypeStruct((RANK, MODEL), F32),
            jax.ShapeDtypeStruct((RANK, WIDTH), F32),
        ),
        in_specs=[smem, vmem, vmem, vmem, vmem],
        out_specs=(smem, hbm, hbm, hbm, hbm),
        scratch_shapes=[
            pltpu.VMEM((2, ROWS, MODEL), BF16),
            pltpu.VMEM((RANK, MODEL), F32),
            pltpu.VMEM((RANK, WIDTH), F32),
            pltpu.SemaphoreType.DMA((4,)),
        ],
        compiler_params=pltpu.CompilerParams(vmem_limit_bytes=32 * 1024 * 1024),
    )(loss, small, mixed, sums, down_rows)
    return (loss[0, 0], first_gradient, second_gradient, grad_down.T, grad_up)


def solution(mesh):
    in_specs = (P(("blk", "grp"), None), P(("blk", "grp"), None), P(("blk", "grp"), None), P(), P())
    out_specs = (P(), P(("blk", "grp"), None), P(("blk", "grp"), None), P(), P())
    return jax.shard_map(shards, mesh=mesh, in_specs=in_specs, out_specs=out_specs, check_vma=False)
```

```python
import jax
import jax.numpy as jnp
from jax import lax
from jax.experimental import pallas as pl
from jax.experimental.pallas import tpu as pltpu
from jax.sharding import PartitionSpec as P

SCALE = 20.0
EPS = 1e-06
MESH = pl.DeviceIdType.MESH
F32 = jnp.float32
BF16 = jnp.bfloat16

ROWS = 128
WIDTH = 1024
MODEL = 4096
RANK = 64
LANES = 128
TEXTS = 16384

ORDER = (0, 1, 2, 4, 3, 6, 5, 7)
SLOT = {mask: slot for slot, mask in enumerate(ORDER)}
BACK = {(7, 0): 1, (7, 1): 4}
BACK.update({(mask, half): link for mask, link in ((6, 2), (3, 1), (5, 4), (1, 1), (2, 2), (4, 4)) for half in (0, 1)})
HALF = ROWS // 2
COPIES = 176
TOTAL = MODEL + WIDTH
HALF_RANK = RANK // 2
PIECE = TOTAL // 8


def nn(a, b):
    return lax.dot_general(a, b, (((1,), (0,)), ((), ())), preferred_element_type=F32)


def nt(a, b):
    return lax.dot_general(a, b, (((1,), (1,)), ((), ())), preferred_element_type=F32)


def tn(a, b):
    return lax.dot_general(a, b, (((0,), (0,)), ((), ())), preferred_element_type=F32)


class Links:
    def __init__(self, send_sems, recv_sems):
        self.send_sems, self.recv_sems, self.count, self.sent = send_sems, recv_sems, 0, []

    def copy(self, src, dst, device):
        index = self.count
        self.count += 1
        made = pltpu.make_async_remote_copy(
            src_ref=src,
            dst_ref=dst,
            send_sem=self.send_sems.at[index],
            recv_sem=self.recv_sems.at[index],
            device_id=device,
            device_id_type=MESH,
        )
        made.start()
        self.sent.append(made)
        return made

    def settle(self, made):
        made.wait_recv()
        made.wait_send()
        self.sent = [copy for copy in self.sent if copy is not made]

    def drain(self):
        for made in self.sent:
            made.wait_send()
        self.sent = []


def half_rows(half):
    return slice(half * HALF, (half + 1) * HALF)


class Group:
    def __init__(self, links, near, data, stride, out, landing, part):
        self.links, self.near, self.data, self.stride = links, near, data, stride
        self.out, self.landing, self.part, self.got, self.back_got = out, landing, part, {}, {}

    def at(self, mask, half):
        first = SLOT[mask] * self.stride + half * HALF
        return self.data.at[first : first + HALF]

    def give(self, mask, half, link):
        there = mask ^ link
        self.got[there, half] = self.links.copy(self.at(mask, half), self.at(there, half), self.near[link])

    def have(self, mask, half):
        self.got[mask, half].wait_recv()

    def back(self, mask, half, add=None):
        rows = half_rows(half)
        value = self.part(mask, rows)
        if add is not None:
            self.back_got[add, half].wait_recv()
            value = value + self.landing[add - 1, rows].astype(F32)
        self.out[mask - 1, rows] = value.astype(BF16)
        self.back_got[mask, half] = self.links.copy(
            self.out.at[mask - 1, rows], self.landing.at[mask - 1, rows], self.near[BACK[mask, half]]
        )

    def whole(self):
        total = self.part(0, slice(0, ROWS))
        for mask in (1, 2, 4):
            for half in (0, 1):
                self.back_got[mask, half].wait_recv()
        for mask in (1, 2, 4):
            total = total + self.landing[mask - 1].astype(F32)
        return total


def body(
    h1_hbm, h2_hbm, partner_hbm, down_hbm, up_hbm,
    loss_ref, g1_hbm, g2_hbm, sums_hbm,
    h, down, up_ref, partner_ref, unit, inv, low, q, k, expo, rowacc, colacc, rows, cols, row_in, row_sib_in, col_in,
    w, colb, pq, pk, sib_out, sib_in, q_out, q_in, k_out, k_in, pos,
    gl, gm, state, gsum, gsend, core_in, plane_out, plane_in, z_all, sums,
    loss_core, loss_plane, loss_z,
    load_sems, send_sems, recv_sems,
):
    blk, grp = lax.axis_index("blk"), lax.axis_index("grp")
    x, z_hi = lax.div(blk, 2), lax.rem(blk, 2)
    z_lo, y, core = lax.div(grp, 8), lax.rem(lax.div(grp, 2), 4), lax.rem(grp, 2)
    z = z_hi * 2 + z_lo
    place = x * 4 + y

    def at(dx=0, dy=0, dz=0, other=False):
        px, py, pz = lax.rem(x + dx, 4), lax.rem(y + dy, 4), lax.rem(z + dz, 4)
        pc = 1 - core if other else core
        return (px * 2 + lax.div(pz, 2), lax.rem(pz, 2) * 8 + py * 2 + pc)

    up_or_down = [1 + 2 * lax.rem(c, 2) for c in (x, y, z)]

    def cube(flip):
        steps = [4 - s if flip else s for s in up_or_down]
        return {m: at(*(s if m & bit else 0 for bit, s in zip((1, 2, 4), steps))) for m in range(1, 8)}

    sibling = at(other=True)
    q_near, k_near = cube(False), cube(True)
    plane = {(dx, dy): at(dx, dy) for dx in range(4) for dy in range(4) if dx or dy}
    column = {dz: at(dz=dz) for dz in (1, 2, 3)}
    links = Links(send_sems, recv_sems)

    loads = [
        pltpu.make_async_copy(h1_hbm, h.at[0:ROWS], load_sems.at[0]),
        pltpu.make_async_copy(h2_hbm, h.at[ROWS : 2 * ROWS], load_sems.at[1]),
        pltpu.make_async_copy(down_hbm, down, load_sems.at[2]),
        pltpu.make_async_copy(up_hbm, up_ref, load_sems.at[3]),
        pltpu.make_async_copy(partner_hbm, partner_ref, load_sems.at[4]),
    ]
    for load in loads:
        load.start()
    partners = [sibling, *(near[m] for near in (q_near, k_near) for m in (1, 2, 4))]
    barrier = pltpu.get_barrier_semaphore()
    for device in partners:
        pl.semaphore_signal(barrier, inc=1, device_id=device, device_id_type=MESH)
    rowacc[...] = jnp.zeros_like(rowacc)
    colacc[...] = jnp.zeros_like(colacc)
    for load in loads:
        load.wait()

    low[...] = nt(h[...], down[...]).astype(BF16)
    for view, own in enumerate((q, k)):
        here = slice(view * ROWS, (view + 1) * ROWS)
        mixed = h[here, 0:WIDTH].astype(F32) + nn(low[here, :], up_ref[...])
        inverse = lax.rsqrt(jnp.sum(mixed * mixed, axis=1, keepdims=True) + EPS)
        inv[here, :] = jnp.broadcast_to(inverse, (ROWS, LANES))
        normal = mixed * inverse
        unit[here, :] = normal
        own[0:ROWS, :] = normal.astype(BF16)
    pl.semaphore_wait(barrier, len(partners))

    sib = {}

    def q_part(mask, here):
        return pq[SLOT[mask], here, :] + sib_in[SLOT[mask], here, :].astype(F32)

    def k_part(mask, here):
        first = SLOT[mask] * ROWS
        return pk[first + here.start : first + here.stop, :]

    queries = Group(links, q_near, q, 2 * ROWS, q_out, q_in, q_part)
    keys = Group(links, k_near, k, ROWS, k_out, k_in, k_part)
    groups = (queries, keys)

    def to_sibling(mask):
        first = SLOT[mask] * 2 * ROWS
        return links.copy(q.at[first : first + ROWS], q.at[first + ROWS : first + 2 * ROWS], sibling)

    FIRST = {1: 0, 2: 1, 4: 0}
    NEXT = {4: 2, 2: 1, 1: 4}
    for turn in (0, 1):
        for group in groups:
            for link in (1, 2, 4):
                group.give(0, FIRST[link] ^ turn, link)
    passed = {0: to_sibling(0)}
    for turn in (0, 1):
        for group in groups:
            for mask in (4, 2, 1):
                group.have(mask, FIRST[mask] ^ turn)
                group.give(mask, FIRST[mask] ^ turn, NEXT[mask])
    for mask in (1, 2, 4):
        passed[mask] = to_sibling(mask)

    def score(first_row, row_count, first_col, col_count):
        def chunk(step, carry):
            here = pl.ds(pl.multiple_of(first_row + step * 256, 256), 256)
            columns = pl.ds(first_col, col_count)
            value = jnp.exp(SCALE * nt(q[here, :], k[columns, :]) - SCALE)
            expo[here, columns] = value
            colacc[:, columns] += jnp.sum(value.reshape(32, 8, col_count), axis=0)
            total = value[:, 0:LANES]
            for lane in range(LANES, col_count, LANES):
                total = total + value[:, lane : lane + LANES]
            rowacc[here, :] += total
            return carry

        lax.fori_loop(0, row_count // 256, chunk, 0)

    for mask in (0, 1, 2, 4):
        passed[mask].wait_recv()
    score(0, 1024, 0, 512)
    for group in groups:
        group.have(6, 0)
        group.give(6, 0, 1)
        group.have(3, 1)
        group.give(3, 1, 4)
    for mask, half in ((6, 1), (3, 0), (5, 0), (5, 1)):
        for group in groups:
            group.have(mask, half)
    for mask in (3, 6, 5):
        passed[mask] = to_sibling(mask)
    score(0, 1024, 512, 256)
    for mask in (3, 6, 5):
        passed[mask].wait_recv()
    score(1024, 768, 0, 768)
    for half in (0, 1):
        queries.have(7, half)
    passed[7] = to_sibling(7)
    for half in (0, 1):
        keys.have(7, half)
    score(0, 1792, 768, 256)
    passed[7].wait_recv()
    score(1792, 256, 0, 1024)
    links.drain()

    for block in range(8):
        cols[block : block + 1, :] = jnp.sum(colacc[:, block * LANES : (block + 1) * LANES], axis=0, keepdims=True)
    col_copies = {m: links.copy(cols, col_in.at[m - 1], k_near[m]) for m in range(1, 8)}
    for block in range(16):
        lanes = rowacc[block * ROWS : (block + 1) * ROWS, :].T
        rows[block : block + 1, :] = jnp.sum(lanes, axis=0, keepdims=True)
    row_swap = links.copy(rows, row_sib_in, sibling)
    links.settle(row_swap)
    for slot in range(8):
        for rank in range(2):
            here, there = slot * 2 + rank, slot * 2 + 1 - rank
            rows[here : here + 1, :] = rows[here : here + 1, :] + row_sib_in[there : there + 1, :]
    row_copies = {m: links.copy(rows, row_in.at[m - 1], q_near[m]) for m in range(1, 8)}

    choice = (lax.broadcasted_iota(jnp.int32, (ROWS, ROWS), 0) == partner_ref[...]).astype(BF16)
    pos[0:ROWS, :] = tn(choice, k[0:ROWS, :])
    pos[ROWS : 2 * ROWS, :] = nn(choice, q[0:ROWS, :])
    positive = SCALE * jnp.sum(q[0:ROWS, :].astype(F32) * pos[0:ROWS, :])

    def cube_sum(total, arrived, copies, width):
        for copy in copies.values():
            links.settle(copy)
        sums = []
        for mask in ORDER:
            value = total[SLOT[mask] * width : (SLOT[mask] + 1) * width, :]
            for m in range(1, 8):
                there = SLOT[mask ^ m] * width
                value = value + arrived[m - 1, there : there + width, :]
            sums.append(value)
        return sums

    sums_of_cols = cube_sum(cols, col_in, col_copies, 1)
    for slot, value in enumerate(sums_of_cols):
        colb[0:1, slot * LANES : (slot + 1) * LANES] = 0.5 / value
    sums_of_rows = cube_sum(rows, row_in, row_copies, 2)
    for slot, value in enumerate(sums_of_rows):
        rows[2 * slot : 2 * slot + 2, :] = 0.5 / value

    def weigh(block, carry):
        here = pl.ds(pl.multiple_of(block * ROWS, ROWS), ROWS)
        row = jnp.broadcast_to(rows[pl.ds(block, 1), :], (ROWS, ROWS)).T
        for lane in range(0, WIDTH, LANES):
            columns = slice(lane, lane + LANES)
            w[here, columns] = (expo[here, columns] * (row + colb[0:1, columns])).astype(BF16)
        return carry

    lax.fori_loop(0, 16, weigh, 0)

    def key_part(first):
        pk[first : first + 256, :] = tn(w[:, first : first + 256], q[...])

    def query_part(mask):
        slot = SLOT[mask]
        here = slot * 2 * ROWS
        part = nn(w[here : here + 2 * ROWS, :], k[...])
        pq[slot, :, :] = part[0:ROWS]
        sib_out[slot, :, :] = part[ROWS:].astype(BF16)
        sib[mask] = links.copy(sib_out.at[slot], sib_in.at[slot], sibling)

    key_part(768)
    for mask, half in ((7, 0), (7, 1), (5, 0), (5, 1)):
        keys.back(mask, half)
    query_part(7)
    key_part(512)
    keys.back(3, 0)
    keys.back(6, 1)
    sib[7].wait_recv()
    queries.back(7, 0)
    queries.back(7, 1)
    for mask in (5, 3, 6):
        query_part(mask)
    sib[5].wait_recv()
    queries.back(5, 0)
    queries.back(5, 1)
    sib[3].wait_recv()
    queries.back(3, 0)
    sib[6].wait_recv()
    queries.back(6, 1)

    terms = 0.5 * jnp.sum(jnp.log(sums_of_rows[0][0:1, :])) + 0.5 * jnp.sum(jnp.log(sums_of_cols[0])) - positive
    loss_core[core, :, :] = jnp.broadcast_to(terms, (8, LANES))
    loss_swap = links.copy(loss_core.at[core], loss_core.at[core], sibling)
    key_part(256)
    keys.back(6, 0, 7)
    keys.back(3, 1, 7)
    for mask in (1, 2, 4):
        query_part(mask)
    loss_swap.wait_recv()
    loss_plane[place, :, :] = jnp.sum(loss_core[...], axis=0)
    loss_copies = [links.copy(loss_plane.at[place], loss_plane.at[place], device) for device in plane.values()]
    queries.back(6, 0, 7)
    queries.back(3, 1, 7)
    key_part(0)
    keys.back(1, 0, 5)
    keys.back(2, 0, 3)
    keys.back(4, 1, 6)
    keys.back(1, 1, 5)
    query_part(0)
    for mask in (1, 2, 4):
        sib[mask].wait_recv()
    queries.back(1, 0, 5)
    queries.back(2, 0, 3)
    queries.back(4, 1, 6)
    queries.back(1, 1, 5)
    keys.back(4, 0, 6)
    keys.back(2, 1, 3)
    queries.back(4, 0, 6)
    queries.back(2, 1, 3)
    sib[0].wait_recv()
    for copy in loss_copies:
        copy.wait_recv()
    loss_z[z, :, :] = jnp.sum(loss_plane[...], axis=0)
    loss_copies = [links.copy(loss_z.at[z], loss_z.at[z], device) for device in column.values()]

    for view, group in ((1, keys), (0, queries)):
        here = slice(view * ROWS, (view + 1) * ROWS)
        gradient = SCALE * (group.whole() - pos[here, :])
        normal = unit[here, :]
        along = jnp.sum(normal * gradient, axis=1, keepdims=True)
        gm[here, :] = (inv[here, 0:1] * (gradient - normal * along)).astype(BF16)
        small = nt(gm[here, :], up_ref[...])
        gl[here, :] = small.astype(BF16)
        small_rows = small.T.astype(BF16)

        def down_chunk(step, carry, here=here, small_rows=small_rows, view=view):
            columns = pl.ds(pl.multiple_of(step * 512, 512), 512)
            value = nn(small_rows, h[here, columns])
            if view == 0:
                value = value + gsum[:, columns]
                gsend[:, columns] = value.astype(BF16)
            gsum[:, columns] = value
            return carry

        lax.fori_loop(0, MODEL // 512, down_chunk, 0)
        value = tn(low[here, :], gm[here, :])
        if view == 0:
            value = value + gsum[:, MODEL:TOTAL]
            gsend[:, MODEL:TOTAL] = value.astype(BF16)
        gsum[:, MODEL:TOTAL] = value

    mine = pl.ds(pl.multiple_of(core * HALF_RANK, HALF_RANK), HALF_RANK)
    theirs = pl.ds(pl.multiple_of((1 - core) * HALF_RANK, HALF_RANK), HALF_RANK)
    core_got = links.copy(gsend.at[theirs], core_in, sibling)
    for copy in loss_copies:
        copy.wait_recv()
    loss_ref[0, 0] = jnp.sum(jnp.sum(loss_z[...], axis=0)[0:1, 0:1]) * (1.0 / TEXTS) + SCALE
    core_got.wait_recv()
    for piece in range(16):
        top, side = (piece // 8) * 16, (piece % 8) * PIECE
        columns = slice(side, side + PIECE)
        value = gsum[pl.ds(pl.multiple_of(core * HALF_RANK + top, 16), 16), columns]
        value = value + core_in[top : top + 16, columns].astype(F32)
        plane_out[piece, :, :] = value.astype(BF16)
    plane_got = []
    for (dx, dy), device in plane.items():
        there = lax.rem(x + dx, 4) * 4 + lax.rem(y + dy, 4)
        plane_got.append(links.copy(plane_out.at[there], plane_in.at[place], device))
    plane_in[place, :, :] = plane_out[place]
    stores = []
    for view, target in enumerate((g1_hbm, g2_hbm)):
        here = slice(view * ROWS, (view + 1) * ROWS)
        state[view, :, 0:WIDTH] = (nn(gl[here, :], down[:, 0:WIDTH]) + gm[here, :].astype(F32)).astype(BF16)

        def chunk(step, carry, here=here, view=view):
            columns = pl.ds(pl.multiple_of(WIDTH + step * 512, 512), 512)
            state[view, :, columns] = nn(gl[here, :], down[:, columns]).astype(BF16)
            return carry

        lax.fori_loop(0, (MODEL - WIDTH) // 512, chunk, 0)
        stores.append(pltpu.make_async_copy(state.at[view], target, load_sems.at[view]))
        stores[-1].start()
    for copy in plane_got:
        copy.wait_recv()
    z_all[z, :, :] = jnp.sum(plane_in[...].astype(F32), axis=0).astype(BF16)
    z_got = [links.copy(z_all.at[z], z_all.at[z], device) for device in column.values()]
    for copy in z_got:
        copy.wait_recv()
    sums[place, :, :] = jnp.sum(z_all[...].astype(F32), axis=0).astype(BF16)
    plane_back = {step: links.copy(sums.at[place], sums.at[place], device) for step, device in plane.items()}
    core_back = [links.copy(sums.at[place], sums_hbm.at[core, place], sibling)]
    for (dx, dy), copy in plane_back.items():
        copy.wait_recv()
        came = lax.rem(x + 4 - dx, 4) * 4 + lax.rem(y + 4 - dy, 4)
        core_back.append(links.copy(sums.at[came], sums_hbm.at[core, came], sibling))
    stores.append(pltpu.make_async_copy(sums, sums_hbm.at[core], load_sems.at[2]))
    stores[-1].start()
    for copy in core_back:
        copy.wait_recv()
    for store in stores:
        store.wait()
    links.drain()


def finish(
    loss_in, g1_in, g2_in, sums_in, loss_out, g1_out, g2_out, gdown_out, gup_out, sums, grad_down, grad_up, sems
):
    load = pltpu.make_async_copy(sums_in, sums, sems.at[0])
    load.start()
    copies = [pltpu.make_async_copy(g1_in, g1_out, sems.at[1]), pltpu.make_async_copy(g2_in, g2_out, sems.at[2])]
    for copy in copies:
        copy.start()
    loss_out[0, 0] = loss_in[0, 0]
    load.wait()
    for rank in range(2):
        for piece in range(16):
            top, first = rank * HALF_RANK + (piece // 8) * 16, (piece % 8) * PIECE
            last = first + PIECE
            value = sums[rank, piece].astype(F32)
            rows = slice(top, top + 16)
            if last <= MODEL:
                grad_down[rows, first:last] = value
            elif first < MODEL:
                grad_down[rows, first:MODEL] = value[:, 0 : MODEL - first]
                grad_up[rows, 0 : last - MODEL] = value[:, MODEL - first :]
            else:
                grad_up[rows, first - MODEL : last - MODEL] = value
    for source, target, index in ((grad_down, gdown_out, 3), (grad_up, gup_out, 4)):
        copies.append(pltpu.make_async_copy(source, target, sems.at[index]))
        copies[-1].start()
    for copy in copies:
        copy.wait()


def shards(first_pooled_view, second_pooled_view, partner, adapter_down_weight, adapter_up_weight):
    hbm = pl.BlockSpec(memory_space=pl.ANY)
    smem = pl.BlockSpec(memory_space=pltpu.SMEM)
    down_rows = adapter_down_weight.T
    loss, first_state, second_state, sums = pl.pallas_call(
        body,
        out_shape=(
            jax.ShapeDtypeStruct((1, 1), F32),
            jax.ShapeDtypeStruct((ROWS, MODEL), BF16),
            jax.ShapeDtypeStruct((ROWS, MODEL), BF16),
            jax.ShapeDtypeStruct((2, 16, 16, PIECE), BF16),
        ),
        in_specs=[hbm, hbm, hbm, hbm, hbm],
        out_specs=(smem, hbm, hbm, hbm),
        scratch_shapes=[
            pltpu.VMEM((2 * ROWS, MODEL), BF16),
            pltpu.VMEM((RANK, MODEL), BF16),
            pltpu.VMEM((RANK, WIDTH), BF16),
            pltpu.VMEM((1, ROWS), jnp.int32),
            pltpu.VMEM((2 * ROWS, WIDTH), F32),
            pltpu.VMEM((2 * ROWS, LANES), F32),
            pltpu.VMEM((2 * ROWS, RANK), BF16),
            pltpu.VMEM((16 * ROWS, WIDTH), BF16),
            pltpu.VMEM((8 * ROWS, WIDTH), BF16),
            pltpu.VMEM((16 * ROWS, 8 * ROWS), F32),
            pltpu.VMEM((16 * ROWS, LANES), F32),
            pltpu.VMEM((8, 8 * ROWS), F32),
            pltpu.VMEM((16, LANES), F32),
            pltpu.VMEM((8, LANES), F32),
            pltpu.VMEM((7, 16, LANES), F32),
            pltpu.VMEM((16, LANES), F32),
            pltpu.VMEM((7, 8, LANES), F32),
            pltpu.VMEM((16 * ROWS, 8 * ROWS), BF16),
            pltpu.VMEM((8, 8 * ROWS), F32),
            pltpu.VMEM((8, ROWS, WIDTH), F32),
            pltpu.VMEM((8 * ROWS, WIDTH), F32),
            pltpu.VMEM((8, ROWS, WIDTH), BF16),
            pltpu.VMEM((8, ROWS, WIDTH), BF16),
            pltpu.VMEM((7, ROWS, WIDTH), BF16),
            pltpu.VMEM((7, ROWS, WIDTH), BF16),
            pltpu.VMEM((7, ROWS, WIDTH), BF16),
            pltpu.VMEM((7, ROWS, WIDTH), BF16),
            pltpu.VMEM((2 * ROWS, WIDTH), F32),
            pltpu.VMEM((2 * ROWS, RANK), BF16),
            pltpu.VMEM((2 * ROWS, WIDTH), BF16),
            pltpu.VMEM((2, ROWS, MODEL), BF16),
            pltpu.VMEM((RANK, TOTAL), F32),
            pltpu.VMEM((RANK, TOTAL), BF16),
            pltpu.VMEM((HALF_RANK, TOTAL), BF16),
            pltpu.VMEM((16, 16, PIECE), BF16),
            pltpu.VMEM((16, 16, PIECE), BF16),
            pltpu.VMEM((4, 16, PIECE), BF16),
            pltpu.VMEM((16, 16, PIECE), BF16),
            pltpu.VMEM((2, 8, LANES), F32),
            pltpu.VMEM((16, 8, LANES), F32),
            pltpu.VMEM((4, 8, LANES), F32),
            pltpu.SemaphoreType.DMA((5,)),
            pltpu.SemaphoreType.DMA((COPIES,)),
            pltpu.SemaphoreType.DMA((COPIES,)),
        ],
        compiler_params=pltpu.CompilerParams(
            collective_id=0, has_side_effects=True, vmem_limit_bytes=60 * 1024 * 1024
        ),
    )(first_pooled_view, second_pooled_view, partner, down_rows, adapter_up_weight)
    loss, first_gradient, second_gradient, grad_down, grad_up = pl.pallas_call(
        finish,
        out_shape=(
            jax.ShapeDtypeStruct((1, 1), F32),
            jax.ShapeDtypeStruct((ROWS, MODEL), BF16),
            jax.ShapeDtypeStruct((ROWS, MODEL), BF16),
            jax.ShapeDtypeStruct((RANK, MODEL), F32),
            jax.ShapeDtypeStruct((RANK, WIDTH), F32),
        ),
        in_specs=[smem, hbm, hbm, hbm],
        out_specs=(smem, hbm, hbm, hbm, hbm),
        scratch_shapes=[
            pltpu.VMEM((2, 16, 16, PIECE), BF16),
            pltpu.VMEM((RANK, MODEL), F32),
            pltpu.VMEM((RANK, WIDTH), F32),
            pltpu.SemaphoreType.DMA((5,)),
        ],
        compiler_params=pltpu.CompilerParams(vmem_limit_bytes=60 * 1024 * 1024),
    )(loss, first_state, second_state, sums)
    return (loss[0, 0], first_gradient, second_gradient, grad_down.T, grad_up)


def solution(mesh):
    in_specs = (P(("blk", "grp"), None), P(("blk", "grp"), None), P(("blk", "grp"), None), P(), P())
    out_specs = (P(), P(("blk", "grp"), None), P(("blk", "grp"), None), P(), P())
    return jax.shard_map(shards, mesh=mesh, in_specs=in_specs, out_specs=out_specs, check_vma=False)
```

```python
import jax
import jax.numpy as jnp
from jax import lax
from jax.experimental import pallas as pl
from jax.experimental.pallas import tpu as pltpu
from jax.sharding import PartitionSpec as P

SCALE = 20.0
EPS = 1e-06
MESH = pl.DeviceIdType.MESH
F32 = jnp.float32
BF16 = jnp.bfloat16

ROWS = 128
WIDTH = 1024
MODEL = 4096
RANK = 64
LANES = 128
TEXTS = 16384

ORDER = (0, 1, 2, 4, 3, 6, 5, 7)
SLOT = {mask: slot for slot, mask in enumerate(ORDER)}
BACK = {(7, 0): 1, (7, 1): 4}
BACK.update({(mask, half): link for mask, link in ((6, 2), (3, 1), (5, 4), (1, 1), (2, 2), (4, 4)) for half in (0, 1)})
HALF = ROWS // 2
COPIES = 176
TOTAL = MODEL + WIDTH
HALF_RANK = RANK // 2
PIECE = TOTAL // 8


def nn(a, b):
    return lax.dot_general(a, b, (((1,), (0,)), ((), ())), preferred_element_type=F32)


def nt(a, b):
    return lax.dot_general(a, b, (((1,), (1,)), ((), ())), preferred_element_type=F32)


def tn(a, b):
    return lax.dot_general(a, b, (((0,), (0,)), ((), ())), preferred_element_type=F32)


class Links:
    def __init__(self, send_sems, recv_sems):
        self.send_sems, self.recv_sems, self.count, self.sent = send_sems, recv_sems, 0, []

    def copy(self, src, dst, device):
        index = self.count
        self.count += 1
        made = pltpu.make_async_remote_copy(
            src_ref=src,
            dst_ref=dst,
            send_sem=self.send_sems.at[index],
            recv_sem=self.recv_sems.at[index],
            device_id=device,
            device_id_type=MESH,
        )
        made.start()
        self.sent.append(made)
        return made

    def settle(self, made):
        made.wait_recv()
        made.wait_send()
        self.sent = [copy for copy in self.sent if copy is not made]

    def drain(self):
        for made in self.sent:
            made.wait_send()
        self.sent = []


def half_rows(half):
    return slice(half * HALF, (half + 1) * HALF)


class Group:
    def __init__(self, links, near, data, stride, out, landing, part):
        self.links, self.near, self.data, self.stride = links, near, data, stride
        self.out, self.landing, self.part, self.got, self.back_got = out, landing, part, {}, {}

    def at(self, mask, half):
        first = SLOT[mask] * self.stride + half * HALF
        return self.data.at[first : first + HALF]

    def give(self, mask, half, link):
        there = mask ^ link
        self.got[there, half] = self.links.copy(self.at(mask, half), self.at(there, half), self.near[link])

    def have(self, mask, half):
        self.got[mask, half].wait_recv()

    def back(self, mask, half, add=None):
        rows = half_rows(half)
        value = self.part(mask, rows)
        if add is not None:
            self.back_got[add, half].wait_recv()
            value = value + self.landing[add - 1, rows].astype(F32)
        self.out[mask - 1, rows] = value.astype(BF16)
        self.back_got[mask, half] = self.links.copy(
            self.out.at[mask - 1, rows], self.landing.at[mask - 1, rows], self.near[BACK[mask, half]]
        )

    def whole(self):
        total = self.part(0, slice(0, ROWS))
        for mask in (1, 2, 4):
            for half in (0, 1):
                self.back_got[mask, half].wait_recv()
        for mask in (1, 2, 4):
            total = total + self.landing[mask - 1].astype(F32)
        return total


def body(
    h1_hbm, h2_hbm, partner_hbm, down_hbm, up_hbm,
    loss_ref, g1_hbm, g2_hbm, sums_hbm,
    h, down, up_ref, partner_ref, unit, inv, low, q, k, expo, rowacc, colacc, rows, cols, row_in, row_sib_in, col_in,
    w, colb, pq, pk, sib_out, sib_in, q_out, q_in, k_out, k_in, pos,
    gl, gm, state, gsum, gsend, core_in, plane_out, plane_in, z_all, sums,
    loss_core, loss_plane, loss_z,
    load_sems, send_sems, recv_sems,
):
    blk, grp = lax.axis_index("blk"), lax.axis_index("grp")
    x, z_hi = lax.div(blk, 2), lax.rem(blk, 2)
    z_lo, y, core = lax.div(grp, 8), lax.rem(lax.div(grp, 2), 4), lax.rem(grp, 2)
    z = z_hi * 2 + z_lo
    place = x * 4 + y

    def at(dx=0, dy=0, dz=0, other=False):
        px, py, pz = lax.rem(x + dx, 4), lax.rem(y + dy, 4), lax.rem(z + dz, 4)
        pc = 1 - core if other else core
        return (px * 2 + lax.div(pz, 2), lax.rem(pz, 2) * 8 + py * 2 + pc)

    up_or_down = [1 + 2 * lax.rem(c, 2) for c in (x, y, z)]

    def cube(flip):
        steps = [4 - s if flip else s for s in up_or_down]
        return {m: at(*(s if m & bit else 0 for bit, s in zip((1, 2, 4), steps))) for m in range(1, 8)}

    sibling = at(other=True)
    q_near, k_near = cube(False), cube(True)
    plane = {(dx, dy): at(dx, dy) for dx in range(4) for dy in range(4) if dx or dy}
    column = {dz: at(dz=dz) for dz in (1, 2, 3)}
    links = Links(send_sems, recv_sems)

    loads = [
        pltpu.make_async_copy(h1_hbm, h.at[0:ROWS], load_sems.at[0]),
        pltpu.make_async_copy(h2_hbm, h.at[ROWS : 2 * ROWS], load_sems.at[1]),
        pltpu.make_async_copy(down_hbm, down, load_sems.at[2]),
        pltpu.make_async_copy(up_hbm, up_ref, load_sems.at[3]),
        pltpu.make_async_copy(partner_hbm, partner_ref, load_sems.at[4]),
    ]
    for load in loads:
        load.start()
    partners = [sibling, *(near[m] for near in (q_near, k_near) for m in (1, 2, 4))]
    barrier = pltpu.get_barrier_semaphore()
    for device in partners:
        pl.semaphore_signal(barrier, inc=1, device_id=device, device_id_type=MESH)
    rowacc[...] = jnp.zeros_like(rowacc)
    colacc[...] = jnp.zeros_like(colacc)
    for load in loads:
        load.wait()

    low[...] = nt(h[...], down[...]).astype(BF16)
    for view, own in enumerate((q, k)):
        here = slice(view * ROWS, (view + 1) * ROWS)
        mixed = h[here, 0:WIDTH].astype(F32) + nn(low[here, :], up_ref[...])
        inverse = lax.rsqrt(jnp.sum(mixed * mixed, axis=1, keepdims=True) + EPS)
        inv[here, :] = jnp.broadcast_to(inverse, (ROWS, LANES))
        normal = mixed * inverse
        unit[here, :] = normal
        own[0:ROWS, :] = normal.astype(BF16)
    pl.semaphore_wait(barrier, len(partners))

    sib = {}

    def q_part(mask, here):
        return pq[SLOT[mask], here, :] + sib_in[SLOT[mask], here, :].astype(F32)

    def k_part(mask, here):
        first = SLOT[mask] * ROWS
        return pk[first + here.start : first + here.stop, :]

    queries = Group(links, q_near, q, 2 * ROWS, q_out, q_in, q_part)
    keys = Group(links, k_near, k, ROWS, k_out, k_in, k_part)
    groups = (queries, keys)

    def to_sibling(mask):
        first = SLOT[mask] * 2 * ROWS
        return links.copy(q.at[first : first + ROWS], q.at[first + ROWS : first + 2 * ROWS], sibling)

    FIRST = {1: 0, 2: 1, 4: 0}
    NEXT = {4: 2, 2: 1, 1: 4}
    for turn in (0, 1):
        for group in groups:
            for link in (1, 2, 4):
                group.give(0, FIRST[link] ^ turn, link)
    passed = {0: to_sibling(0)}
    for turn in (0, 1):
        for group in groups:
            for mask in (4, 2, 1):
                group.have(mask, FIRST[mask] ^ turn)
                group.give(mask, FIRST[mask] ^ turn, NEXT[mask])
    for mask in (1, 2, 4):
        passed[mask] = to_sibling(mask)

    def score(first_row, row_count, first_col, col_count):
        columns = slice(first_col, first_col + col_count)
        for top in range(first_row, first_row + row_count, 512):
            here = slice(top, min(top + 512, first_row + row_count))
            value = jnp.exp(SCALE * nt(q[here, :], k[columns, :]) - SCALE)
            expo[here, columns] = value
            colacc[:, columns] += jnp.sum(value.reshape(-1, 8, col_count), axis=0)
            total = value[:, 0:LANES]
            for lane in range(LANES, col_count, LANES):
                total = total + value[:, lane : lane + LANES]
            rowacc[here, :] += total

    for mask in (0, 1, 2, 4):
        passed[mask].wait_recv()
    score(0, 1024, 0, 512)
    for group in groups:
        group.have(6, 0)
        group.give(6, 0, 1)
        group.have(3, 1)
        group.give(3, 1, 4)
    for mask, half in ((6, 1), (3, 0), (5, 0), (5, 1)):
        for group in groups:
            group.have(mask, half)
    for mask in (3, 6, 5):
        passed[mask] = to_sibling(mask)
    score(0, 1024, 512, 256)
    for mask in (3, 6, 5):
        passed[mask].wait_recv()
    score(1024, 768, 0, 768)
    for half in (0, 1):
        queries.have(7, half)
    passed[7] = to_sibling(7)
    for half in (0, 1):
        keys.have(7, half)
    score(0, 1792, 768, 256)
    passed[7].wait_recv()
    score(1792, 256, 0, 1024)
    links.drain()

    for block in range(8):
        cols[block : block + 1, :] = jnp.sum(colacc[:, block * LANES : (block + 1) * LANES], axis=0, keepdims=True)
    col_copies = {m: links.copy(cols, col_in.at[m - 1], k_near[m]) for m in range(1, 8)}
    for block in range(16):
        lanes = rowacc[block * ROWS : (block + 1) * ROWS, :].T
        rows[block : block + 1, :] = jnp.sum(lanes, axis=0, keepdims=True)
    row_swap = links.copy(rows, row_sib_in, sibling)
    links.settle(row_swap)
    for slot in range(8):
        for rank in range(2):
            here, there = slot * 2 + rank, slot * 2 + 1 - rank
            rows[here : here + 1, :] = rows[here : here + 1, :] + row_sib_in[there : there + 1, :]
    row_copies = {m: links.copy(rows, row_in.at[m - 1], q_near[m]) for m in range(1, 8)}

    choice = (lax.broadcasted_iota(jnp.int32, (ROWS, ROWS), 0) == partner_ref[...]).astype(BF16)
    pos[0:ROWS, :] = tn(choice, k[0:ROWS, :])
    pos[ROWS : 2 * ROWS, :] = nn(choice, q[0:ROWS, :])
    positive = SCALE * jnp.sum(q[0:ROWS, :].astype(F32) * pos[0:ROWS, :])

    def cube_sum(total, arrived, copies, width):
        for copy in copies.values():
            links.settle(copy)
        sums = []
        for mask in ORDER:
            value = total[SLOT[mask] * width : (SLOT[mask] + 1) * width, :]
            for m in range(1, 8):
                there = SLOT[mask ^ m] * width
                value = value + arrived[m - 1, there : there + width, :]
            sums.append(value)
        return sums

    sums_of_cols = cube_sum(cols, col_in, col_copies, 1)
    for slot, value in enumerate(sums_of_cols):
        colb[0:1, slot * LANES : (slot + 1) * LANES] = 0.5 / value
    sums_of_rows = cube_sum(rows, row_in, row_copies, 2)
    for slot, value in enumerate(sums_of_rows):
        rows[2 * slot : 2 * slot + 2, :] = 0.5 / value

    def weigh(step, carry):
        for part in range(2):
            block = step * 2 + part
            here = pl.ds(pl.multiple_of(block * ROWS, ROWS), ROWS)
            row = jnp.broadcast_to(rows[pl.ds(block, 1), :], (ROWS, ROWS)).T
            for lane in range(0, WIDTH, LANES):
                columns = slice(lane, lane + LANES)
                w[here, columns] = (expo[here, columns] * (row + colb[0:1, columns])).astype(BF16)
        return carry

    lax.fori_loop(0, 8, weigh, 0)

    def key_part(first):
        pk[first : first + 256, :] = tn(w[:, first : first + 256], q[...])

    def query_part(mask):
        slot = SLOT[mask]
        here = slot * 2 * ROWS
        part = nn(w[here : here + 2 * ROWS, :], k[...])
        pq[slot, :, :] = part[0:ROWS]
        sib_out[slot, :, :] = part[ROWS:].astype(BF16)
        sib[mask] = links.copy(sib_out.at[slot], sib_in.at[slot], sibling)

    query_part(7)
    key_part(768)
    for mask, half in ((7, 0), (7, 1), (5, 0), (5, 1)):
        keys.back(mask, half)
    sib[7].wait_recv()
    queries.back(7, 0)
    queries.back(7, 1)
    for mask in (5, 3, 6):
        query_part(mask)
    key_part(512)
    keys.back(3, 0)
    keys.back(6, 1)
    sib[5].wait_recv()
    queries.back(5, 0)
    queries.back(5, 1)
    sib[3].wait_recv()
    queries.back(3, 0)
    sib[6].wait_recv()
    queries.back(6, 1)

    key_part(256)
    keys.back(6, 0, 7)
    keys.back(3, 1, 7)
    queries.back(6, 0, 7)
    queries.back(3, 1, 7)
    for mask in (1, 2, 4):
        query_part(mask)
    key_part(0)
    for mask in (1, 2, 4):
        sib[mask].wait_recv()
    for mask, half, add in ((1, 0, 5), (2, 0, 3), (4, 1, 6), (1, 1, 5), (4, 0, 6), (2, 1, 3)):
        for group in groups:
            group.back(mask, half, add)
    query_part(0)

    terms = 0.5 * jnp.sum(jnp.log(sums_of_rows[0][0:1, :])) + 0.5 * jnp.sum(jnp.log(sums_of_cols[0])) - positive
    loss_core[core, :, :] = jnp.broadcast_to(terms, (8, LANES))
    loss_swap = links.copy(loss_core.at[core], loss_core.at[core], sibling)
    loss_swap.wait_recv()
    loss_plane[place, :, :] = jnp.sum(loss_core[...], axis=0)
    sib[0].wait_recv()

    for view, group in ((1, keys), (0, queries)):
        here = slice(view * ROWS, (view + 1) * ROWS)
        gradient = SCALE * (group.whole() - pos[here, :])
        normal = unit[here, :]
        along = jnp.sum(normal * gradient, axis=1, keepdims=True)
        gm[here, :] = (inv[here, 0:1] * (gradient - normal * along)).astype(BF16)
        small = nt(gm[here, :], up_ref[...])
        gl[here, :] = small.astype(BF16)
        small_rows = small.T.astype(BF16)
        for first in range(0, TOTAL, WIDTH):
            columns = slice(first, first + WIDTH)
            value = nn(small_rows, h[here, columns]) if first < MODEL else tn(low[here, :], gm[here, :])
            if view == 0:
                value = value + gsum[:, columns]
                gsend[:, columns] = value.astype(BF16)
            gsum[:, columns] = value

    mine = pl.ds(pl.multiple_of(core * HALF_RANK, HALF_RANK), HALF_RANK)
    theirs = pl.ds(pl.multiple_of((1 - core) * HALF_RANK, HALF_RANK), HALF_RANK)
    core_got = links.copy(gsend.at[theirs], core_in, sibling)
    core_got.wait_recv()
    for piece in range(16):
        top, side = (piece // 8) * 16, (piece % 8) * PIECE
        columns = slice(side, side + PIECE)
        value = gsum[pl.ds(pl.multiple_of(core * HALF_RANK + top, 16), 16), columns]
        value = value + core_in[top : top + 16, columns].astype(F32)
        plane_out[piece, :, :] = value.astype(BF16)
    plane_got = []
    for (dx, dy), device in plane.items():
        there = lax.rem(x + dx, 4) * 4 + lax.rem(y + dy, 4)
        plane_got.append(links.copy(plane_out.at[there], plane_in.at[place], device))
    plane_in[place, :, :] = plane_out[place]
    loss_got = [links.copy(loss_plane.at[place], loss_plane.at[place], device) for device in plane.values()]
    stores = []
    for view, target in enumerate((g1_hbm, g2_hbm)):
        here = slice(view * ROWS, (view + 1) * ROWS)
        state[view, :, 0:WIDTH] = (nn(gl[here, :], down[:, 0:WIDTH]) + gm[here, :].astype(F32)).astype(BF16)

        def chunk(step, carry, here=here, view=view):
            columns = pl.ds(pl.multiple_of(WIDTH + step * 512, 512), 512)
            state[view, :, columns] = nn(gl[here, :], down[:, columns]).astype(BF16)
            return carry

        lax.fori_loop(0, (MODEL - WIDTH) // 512, chunk, 0)
        stores.append(pltpu.make_async_copy(state.at[view], target, load_sems.at[view]))
        stores[-1].start()
    for copy in plane_got:
        copy.wait_recv()
    z_all[z, :, :] = jnp.sum(plane_in[...].astype(F32), axis=0).astype(BF16)
    z_got = [links.copy(z_all.at[z], z_all.at[z], device) for device in column.values()]
    for copy in loss_got:
        copy.wait_recv()
    loss_z[z, :, :] = jnp.sum(loss_plane[...], axis=0)
    loss_got = [links.copy(loss_z.at[z], loss_z.at[z], device) for device in column.values()]
    for copy in z_got:
        copy.wait_recv()
    sums[place, :, :] = jnp.sum(z_all[...].astype(F32), axis=0).astype(BF16)
    plane_back = {step: links.copy(sums.at[place], sums.at[place], device) for step, device in plane.items()}
    core_back = [links.copy(sums.at[place], sums_hbm.at[core, place], sibling)]
    for copy in loss_got:
        copy.wait_recv()
    loss_ref[0, 0] = jnp.sum(jnp.sum(loss_z[...], axis=0)[0:1, 0:1]) * (1.0 / TEXTS) + SCALE
    for (dx, dy), copy in plane_back.items():
        copy.wait_recv()
        came = lax.rem(x + 4 - dx, 4) * 4 + lax.rem(y + 4 - dy, 4)
        core_back.append(links.copy(sums.at[came], sums_hbm.at[core, came], sibling))
    stores.append(pltpu.make_async_copy(sums, sums_hbm.at[core], load_sems.at[2]))
    stores[-1].start()
    for copy in core_back:
        copy.wait_recv()
    for store in stores:
        store.wait()
    links.drain()


def finish(
    loss_in, g1_in, g2_in, sums_in, loss_out, g1_out, g2_out, gdown_out, gup_out, g1, g2, sums, grad_down, grad_up, sems
):
    def copy(source, target, index):
        made = pltpu.make_async_copy(source, target, sems.at[index])
        made.start()
        return made

    first = copy(sums_in, sums, 0)
    pieces = []
    for source, buffer, target in ((g1_in, g1, g1_out), (g2_in, g2, g2_out)):
        for top in range(0, ROWS, ROWS // 4):
            here = pl.ds(top, ROWS // 4)
            pieces.append((copy(source.at[here], buffer.at[here], 1 + len(pieces)), buffer.at[here], target.at[here]))
    loss_out[0, 0] = loss_in[0, 0]
    stores = []
    first.wait()
    for rank in range(2):
        for piece in range(16):
            top, start = rank * HALF_RANK + (piece // 8) * 16, (piece % 8) * PIECE
            last = start + PIECE
            value = sums[rank, piece].astype(F32)
            rows = slice(top, top + 16)
            if last <= MODEL:
                grad_down[rows, start:last] = value
            elif start < MODEL:
                grad_down[rows, start:MODEL] = value[:, 0 : MODEL - start]
                grad_up[rows, 0 : last - MODEL] = value[:, MODEL - start :]
            else:
                grad_up[rows, start - MODEL : last - MODEL] = value
        rows = pl.ds(rank * HALF_RANK, HALF_RANK)
        stores.append(copy(grad_down.at[rows], gdown_out.at[rows], 17 + 2 * rank))
        stores.append(copy(grad_up.at[rows], gup_out.at[rows], 18 + 2 * rank))
    for index, (load, buffer, target) in enumerate(pieces):
        load.wait()
        stores.append(copy(buffer, target, 9 + index))
    for store in stores:
        store.wait()


def shards(first_pooled_view, second_pooled_view, partner, adapter_down_weight, adapter_up_weight):
    hbm = pl.BlockSpec(memory_space=pl.ANY)
    smem = pl.BlockSpec(memory_space=pltpu.SMEM)
    down_rows = adapter_down_weight.T
    loss, first_state, second_state, sums = pl.pallas_call(
        body,
        out_shape=(
            jax.ShapeDtypeStruct((1, 1), F32),
            jax.ShapeDtypeStruct((ROWS, MODEL), BF16),
            jax.ShapeDtypeStruct((ROWS, MODEL), BF16),
            jax.ShapeDtypeStruct((2, 16, 16, PIECE), BF16),
        ),
        in_specs=[hbm, hbm, hbm, hbm, hbm],
        out_specs=(smem, hbm, hbm, hbm),
        scratch_shapes=[
            pltpu.VMEM((2 * ROWS, MODEL), BF16),
            pltpu.VMEM((RANK, MODEL), BF16),
            pltpu.VMEM((RANK, WIDTH), BF16),
            pltpu.VMEM((1, ROWS), jnp.int32),
            pltpu.VMEM((2 * ROWS, WIDTH), F32),
            pltpu.VMEM((2 * ROWS, LANES), F32),
            pltpu.VMEM((2 * ROWS, RANK), BF16),
            pltpu.VMEM((16 * ROWS, WIDTH), BF16),
            pltpu.VMEM((8 * ROWS, WIDTH), BF16),
            pltpu.VMEM((16 * ROWS, 8 * ROWS), F32),
            pltpu.VMEM((16 * ROWS, LANES), F32),
            pltpu.VMEM((8, 8 * ROWS), F32),
            pltpu.VMEM((16, LANES), F32),
            pltpu.VMEM((8, LANES), F32),
            pltpu.VMEM((7, 16, LANES), F32),
            pltpu.VMEM((16, LANES), F32),
            pltpu.VMEM((7, 8, LANES), F32),
            pltpu.VMEM((16 * ROWS, 8 * ROWS), BF16),
            pltpu.VMEM((8, 8 * ROWS), F32),
            pltpu.VMEM((8, ROWS, WIDTH), F32),
            pltpu.VMEM((8 * ROWS, WIDTH), F32),
            pltpu.VMEM((8, ROWS, WIDTH), BF16),
            pltpu.VMEM((8, ROWS, WIDTH), BF16),
            pltpu.VMEM((7, ROWS, WIDTH), BF16),
            pltpu.VMEM((7, ROWS, WIDTH), BF16),
            pltpu.VMEM((7, ROWS, WIDTH), BF16),
            pltpu.VMEM((7, ROWS, WIDTH), BF16),
            pltpu.VMEM((2 * ROWS, WIDTH), F32),
            pltpu.VMEM((2 * ROWS, RANK), BF16),
            pltpu.VMEM((2 * ROWS, WIDTH), BF16),
            pltpu.VMEM((2, ROWS, MODEL), BF16),
            pltpu.VMEM((RANK, TOTAL), F32),
            pltpu.VMEM((RANK, TOTAL), BF16),
            pltpu.VMEM((HALF_RANK, TOTAL), BF16),
            pltpu.VMEM((16, 16, PIECE), BF16),
            pltpu.VMEM((16, 16, PIECE), BF16),
            pltpu.VMEM((4, 16, PIECE), BF16),
            pltpu.VMEM((16, 16, PIECE), BF16),
            pltpu.VMEM((2, 8, LANES), F32),
            pltpu.VMEM((16, 8, LANES), F32),
            pltpu.VMEM((4, 8, LANES), F32),
            pltpu.SemaphoreType.DMA((5,)),
            pltpu.SemaphoreType.DMA((COPIES,)),
            pltpu.SemaphoreType.DMA((COPIES,)),
        ],
        compiler_params=pltpu.CompilerParams(
            collective_id=0, has_side_effects=True, vmem_limit_bytes=60 * 1024 * 1024
        ),
    )(first_pooled_view, second_pooled_view, partner, down_rows, adapter_up_weight)
    loss, first_gradient, second_gradient, grad_down, grad_up = pl.pallas_call(
        finish,
        out_shape=(
            jax.ShapeDtypeStruct((1, 1), F32),
            jax.ShapeDtypeStruct((ROWS, MODEL), BF16),
            jax.ShapeDtypeStruct((ROWS, MODEL), BF16),
            jax.ShapeDtypeStruct((RANK, MODEL), F32),
            jax.ShapeDtypeStruct((RANK, WIDTH), F32),
        ),
        in_specs=[smem, hbm, hbm, hbm],
        out_specs=(smem, hbm, hbm, hbm, hbm),
        scratch_shapes=[
            pltpu.VMEM((ROWS, MODEL), BF16),
            pltpu.VMEM((ROWS, MODEL), BF16),
            pltpu.VMEM((2, 16, 16, PIECE), BF16),
            pltpu.VMEM((RANK, MODEL), F32),
            pltpu.VMEM((RANK, WIDTH), F32),
            pltpu.SemaphoreType.DMA((21,)),
        ],
        compiler_params=pltpu.CompilerParams(vmem_limit_bytes=60 * 1024 * 1024),
    )(loss, first_state, second_state, sums)
    return (loss[0, 0], first_gradient, second_gradient, grad_down.T, grad_up)


def solution(mesh):
    in_specs = (P(("blk", "grp"), None), P(("blk", "grp"), None), P(("blk", "grp"), None), P(), P())
    out_specs = (P(), P(("blk", "grp"), None), P(("blk", "grp"), None), P(), P())
    return jax.shard_map(shards, mesh=mesh, in_specs=in_specs, out_specs=out_specs, check_vma=False)
```

```python
import jax
import jax.numpy as jnp
from jax import lax
from jax.experimental import pallas as pl
from jax.experimental.pallas import tpu as pltpu
from jax.sharding import PartitionSpec as P

SCALE = 20.0
EPS = 1e-06
MESH = pl.DeviceIdType.MESH
F32 = jnp.float32
BF16 = jnp.bfloat16

ROWS = 128
WIDTH = 1024
MODEL = 4096
RANK = 64
LANES = 128
TEXTS = 16384

ORDER = (0, 1, 2, 4, 3, 6, 5, 7)
SLOT = {mask: slot for slot, mask in enumerate(ORDER)}
BACK = {(7, 0): 1, (7, 1): 4}
BACK.update({(mask, half): link for mask, link in ((6, 2), (3, 1), (5, 4), (1, 1), (2, 2), (4, 4)) for half in (0, 1)})
AFTER = {(6, 0): 7, (3, 1): 7}
AFTER.update({(mask, half): add for mask, add in ((1, 5), (2, 3), (4, 6)) for half in (0, 1)})
STEPS = (
    "Wc", "W7", "Q7", "K7", "k71", "k70", "K5", "q71", "Wr", "q70", "k50", "Q3", "k51", "Q6", "Q5", "K6", "k61",
    "q30", "q61", "K3", "k30", "q50", "Q2", "k31", "Q4", "q60", "q31", "k60", "q51", "Q1", "K1", "K2", "K4", "q41",
    "k10", "q20", "k20", "q10", "k41", "k11", "q40", "k40", "q21", "k21", "q11", "K0", "Q0",
)
SPANS = {"low": (0, 64), "high": (64, 128), "mid": (32, 96), "bottom": (0, 32), "top": (96, 128)}
SPANS.update({"first": (0, 48), "second": (48, 80), "third": (80, 128)})
TURNS = {4: (("low",), ("high",)), 2: (("high",), ("low",)), 1: (("mid",), ("bottom", "top"))}
NEXT = {4: 2, 2: 1, 1: 4}
CORNER = ((6, 4, "first", 1), (3, 2, "third", 4), (5, 1, "second", 2))
HALF = ROWS // 2
SENDS, ARRIVALS = 14, 98
OF_QUERIES, OF_KEYS, TO_CORE, OF_ROWS, OF_COLS, ROW_SWAP, CORE, PLANE, LOSS_PLANE, COLUMN, LOSS_COLUMN, PLANE_BACK, CORE_BACK, LOSS_SWAP = range(SENDS)
TOTAL = MODEL + WIDTH
HALF_RANK = RANK // 2
PIECE = TOTAL // 8


def nn(a, b):
    return lax.dot_general(a, b, (((1,), (0,)), ((), ())), preferred_element_type=F32)


def nt(a, b):
    return lax.dot_general(a, b, (((1,), (1,)), ((), ())), preferred_element_type=F32)


def tn(a, b):
    return lax.dot_general(a, b, (((0,), (0,)), ((), ())), preferred_element_type=F32)


class Links:
    def __init__(self, send_sems, recv_sems, device):
        self.send_sems, self.recv_sems, self.device, self.count = send_sems, recv_sems, device, 0

    def slot(self):
        self.count += 1
        return self.count - 1

    def make(self, src, dst, device, batch, slot):
        return pltpu.make_async_remote_copy(
            src_ref=src,
            dst_ref=dst,
            send_sem=self.send_sems.at[batch],
            recv_sem=self.recv_sems.at[slot],
            device_id=device,
            device_id_type=MESH,
        )

    def copy(self, src, dst, device, batch, slot=None):
        made = self.make(src, dst, device, batch, self.slot() if slot is None else slot)
        made.start()
        return made

    def sent(self, batch, whole):
        self.make(whole, whole, self.device, batch, 0).wait_send()

    def arrived(self, slot, whole):
        self.make(whole, whole, self.device, 0, slot).wait_recv()


def half_rows(half):
    return slice(half * HALF, (half + 1) * HALF)


class Group:
    def __init__(self, links, near, data, stride, out, landing, part, ready, batch):
        self.links, self.near, self.data, self.stride, self.ready, self.batch = links, near, data, stride, ready, batch
        self.out, self.landing, self.part, self.got, self.back_got = out, landing, part, {}, {}

    def at(self, mask, part):
        first, last = SPANS[part]
        return self.data.at[SLOT[mask] * self.stride + first : SLOT[mask] * self.stride + last]

    def give(self, mask, part, link):
        there = mask ^ link
        self.got[there, part] = self.links.copy(self.at(mask, part), self.at(there, part), self.near[link], self.batch)

    def have(self, mask, part):
        self.got[mask, part].wait_recv()

    def back(self, mask, half):
        rows, add = half_rows(half), AFTER.get((mask, half))
        if add is not None:
            self.back_got[add, half].wait_recv()
            value = self.part(mask, rows) + self.landing[add - 1, rows].astype(F32)
            self.out[mask - 1, rows] = value.astype(BF16)
        elif not self.ready:
            self.out[mask - 1, rows] = self.part(mask, rows).astype(BF16)
        self.back_got[mask, half] = self.links.copy(
            self.out.at[mask - 1, rows], self.landing.at[mask - 1, rows], self.near[BACK[mask, half]], self.batch
        )

    def whole(self):
        total = self.part(0, slice(0, ROWS))
        for mask in (1, 2, 4):
            for half in (0, 1):
                self.back_got[mask, half].wait_recv()
        for mask in (1, 2, 4):
            total = total + self.landing[mask - 1].astype(F32)
        return total


def body(
    h1_hbm, h2_hbm, partner_hbm, down_hbm, up_hbm,
    loss_ref, g1_hbm, g2_hbm, sums_hbm,
    h, down, up_ref, partner_ref, unit, inv, low, q, k, expo, rowacc, colacc, rows, cols, row_in, row_sib_in, col_in,
    w, colb, pq, pk, sib_out, sib_in, q_out, q_in, k_out, k_in, pos,
    gl, gm, state, gsum, gsend, core_in, plane_out, plane_in, z_all, sums,
    loss_core, loss_plane, loss_z,
    load_sems, send_sems, recv_sems,
):
    blk, grp = lax.axis_index("blk"), lax.axis_index("grp")
    x, z_hi = lax.div(blk, 2), lax.rem(blk, 2)
    z_lo, y, core = lax.div(grp, 8), lax.rem(lax.div(grp, 2), 4), lax.rem(grp, 2)
    z = z_hi * 2 + z_lo
    place = x * 4 + y

    def at(dx=0, dy=0, dz=0, other=False):
        px, py, pz = lax.rem(x + dx, 4), lax.rem(y + dy, 4), lax.rem(z + dz, 4)
        pc = 1 - core if other else core
        return (px * 2 + lax.div(pz, 2), lax.rem(pz, 2) * 8 + py * 2 + pc)

    up_or_down = [1 + 2 * lax.rem(c, 2) for c in (x, y, z)]

    def cube(flip):
        steps = [4 - s if flip else s for s in up_or_down]
        return {m: at(*(s if m & bit else 0 for bit, s in zip((1, 2, 4), steps))) for m in range(1, 8)}

    sibling = at(other=True)
    q_near, k_near = cube(False), cube(True)
    far_first = sorted(((dx, dy) for dx in range(4) for dy in range(4) if dx or dy), key=lambda d: -sum(min(c, 4 - c) for c in d))
    plane = {step: at(*step) for step in far_first}
    column = {dz: at(dz=dz) for dz in (1, 2, 3)}
    links = Links(send_sems, recv_sems, sibling)

    loads = [
        pltpu.make_async_copy(down_hbm, down, load_sems.at[2]),
        pltpu.make_async_copy(h1_hbm, h.at[0:ROWS], load_sems.at[0]),
        pltpu.make_async_copy(up_hbm, up_ref, load_sems.at[3]),
        pltpu.make_async_copy(h2_hbm, h.at[ROWS : 2 * ROWS], load_sems.at[1]),
        pltpu.make_async_copy(partner_hbm, partner_ref, load_sems.at[4]),
    ]
    for load in loads:
        load.start()
    partners = [sibling, *(near[m] for near in (q_near, k_near) for m in (1, 2, 4))]
    barrier = pltpu.get_barrier_semaphore()
    for device in partners:
        pl.semaphore_signal(barrier, inc=1, device_id=device, device_id_type=MESH)
    rowacc[...] = jnp.zeros_like(rowacc)
    colacc[...] = jnp.zeros_like(colacc)

    for view, own in enumerate((q, k)):
        here = slice(view * ROWS, (view + 1) * ROWS)
        for load in loads[3 * view : 3 * view + 3]:
            load.wait()
        low[here, :] = nt(h[here, :], down[...]).astype(BF16)
        mixed = h[here, 0:WIDTH].astype(F32) + nn(low[here, :], up_ref[...])
        inverse = lax.rsqrt(jnp.sum(mixed * mixed, axis=1, keepdims=True) + EPS)
        inv[here, :] = jnp.broadcast_to(inverse, (ROWS, LANES))
        normal = mixed * inverse
        unit[here, :] = normal
        own[0:ROWS, :] = normal.astype(BF16)
    pl.semaphore_wait(barrier, len(partners))

    sib = {}

    def q_part(mask, here):
        return pq[SLOT[mask], here, :] + sib_in[SLOT[mask], here, :].astype(F32)

    def k_part(mask, here):
        first = SLOT[mask] * ROWS
        return pk[first + here.start : first + here.stop, :]

    queries = Group(links, q_near, q, 2 * ROWS, q_out, q_in, q_part, False, OF_QUERIES)
    keys = Group(links, k_near, k, ROWS, k_out, k_in, k_part, True, OF_KEYS)
    groups = (queries, keys)

    BATCH = {0: 0, 1: 0, 2: 0, 4: 0, 3: 1, 6: 1, 5: 1, 7: 2}
    core_slots = [links.slot() for _ in range(3)]

    def to_sibling(mask, first, last):
        top = SLOT[mask] * 2 * ROWS
        here, there = q.at[top + first : top + last], q.at[top + ROWS + first : top + ROWS + last]
        links.copy(here, there, sibling, TO_CORE, core_slots[BATCH[mask]])

    def sibling_has(batch, shards_of):
        links.arrived(core_slots[batch], q.at[0 : shards_of * ROWS])

    for turn in (0, 1):
        for group in groups:
            for link in (4, 2, 1):
                for part in TURNS[link][turn]:
                    group.give(0, part, link)
    to_sibling(0, 0, ROWS)
    for turn in (0, 1):
        for group in groups:
            for mask in (4, 2, 1):
                for part in TURNS[mask][turn]:
                    group.have(mask, part)
                    group.give(mask, part, NEXT[mask])
                    if group is queries:
                        to_sibling(mask, *SPANS[part])

    def score(first_row, row_count, first_col, col_count):
        columns = slice(first_col, first_col + col_count)
        for top in range(first_row, first_row + row_count, 512):
            here = slice(top, min(top + 512, first_row + row_count))
            value = jnp.exp(SCALE * nt(q[here, :], k[columns, :]) - SCALE)
            expo[here, columns] = value
            colacc[:, columns] += jnp.sum(value.reshape(-1, 8, col_count), axis=0)
            total = value[:, 0:LANES]
            for lane in range(LANES, col_count, LANES):
                total = total + value[:, lane : lane + LANES]
            rowacc[here, :] += total

    sibling_has(0, 4)
    score(0, 1024, 0, 512)
    for turn in (0, 1):
        for group in groups:
            for mask, kind, corner, link in CORNER:
                for part in TURNS[kind][turn]:
                    group.have(mask, part)
                    if group is queries:
                        to_sibling(mask, *SPANS[part])
                if turn == 0:
                    group.give(mask, corner, link)
    score(0, 1024, 512, 256)
    sibling_has(1, 3)
    score(1024, 768, 0, 768)
    for corner in ("first", "second", "third"):
        queries.have(7, corner)
        to_sibling(7, *SPANS[corner])
    for corner in ("first", "second", "third"):
        keys.have(7, corner)
    score(0, 1792, 768, 256)
    sibling_has(2, 1)
    score(1792, 256, 0, 1024)
    links.sent(OF_QUERIES, q.at[0 : 7 * ROWS])
    links.sent(OF_KEYS, k.at[0 : 7 * ROWS])
    links.sent(TO_CORE, q.at[0 : 8 * ROWS])


    for block in range(8):
        cols[block : block + 1, :] = jnp.sum(colacc[:, block * LANES : (block + 1) * LANES], axis=0, keepdims=True)
    col_slot = links.slot()
    for m in (7, 6, 5, 3, 4, 2, 1):
        links.copy(cols, col_in.at[m - 1], k_near[m], OF_COLS, col_slot)
    for block in range(16):
        lanes = rowacc[block * ROWS : (block + 1) * ROWS, :].T
        rows[block : block + 1, :] = jnp.sum(lanes, axis=0, keepdims=True)
    row_swap = links.copy(rows, row_sib_in, sibling, ROW_SWAP)
    row_swap.wait()
    for slot in range(8):
        for rank in range(2):
            here, there = slot * 2 + rank, slot * 2 + 1 - rank
            rows[here : here + 1, :] = rows[here : here + 1, :] + row_sib_in[there : there + 1, :]
    row_slot = links.slot()
    for m in (7, 6, 5, 3, 4, 2, 1):
        links.copy(rows, row_in.at[m - 1], q_near[m], OF_ROWS, row_slot)

    choice = (lax.broadcasted_iota(jnp.int32, (ROWS, ROWS), 0) == partner_ref[...]).astype(BF16)
    pos[0:ROWS, :] = tn(choice, k[0:ROWS, :])
    pos[ROWS : 2 * ROWS, :] = nn(choice, q[0:ROWS, :])
    positive = SCALE * jnp.sum(q[0:ROWS, :].astype(F32) * pos[0:ROWS, :])

    def cube_sum(total, arrived, batch, slot, width):
        links.arrived(slot, arrived)
        links.sent(batch, arrived)
        sums = []
        for mask in ORDER:
            value = total[SLOT[mask] * width : (SLOT[mask] + 1) * width, :]
            for m in range(1, 8):
                there = SLOT[mask ^ m] * width
                value = value + arrived[m - 1, there : there + width, :]
            sums.append(value)
        return sums

    sums_of_cols = cube_sum(cols, col_in, OF_COLS, col_slot, 1)
    for slot, value in enumerate(sums_of_cols):
        colb[0:1, slot * LANES : (slot + 1) * LANES] = 0.5 / value
    sums_of_rows = cube_sum(rows, row_in, OF_ROWS, row_slot, 2)
    for slot, value in enumerate(sums_of_rows):
        rows[2 * slot : 2 * slot + 2, :] = 0.5 / value

    def weigh(first_block, count, first_lane, last_lane):
        def blocks(step, carry):
            for part in range(2):
                block = first_block + step * 2 + part
                here = pl.ds(pl.multiple_of(block * ROWS, ROWS), ROWS)
                row = jnp.broadcast_to(rows[pl.ds(block, 1), :], (ROWS, ROWS)).T
                for lane in range(first_lane, last_lane, LANES):
                    columns = slice(lane, lane + LANES)
                    w[here, columns] = (expo[here, columns] * (row + colb[0:1, columns])).astype(BF16)
            return carry

        lax.fori_loop(0, count // 2, blocks, 0)

    def key_part(mask):
        first = SLOT[mask] * ROWS
        value = tn(w[:, first : first + ROWS], q[...])
        for half in (0, 1):
            here = half_rows(half)
            if mask and (mask, half) not in AFTER:
                k_out[mask - 1, here, :] = value[here].astype(BF16)
            else:
                pk[first + here.start : first + here.stop, :] = value[here]

    def query_part(mask):
        slot = SLOT[mask]
        here = slot * 2 * ROWS
        part = nn(w[here : here + 2 * ROWS, :], k[...])
        pq[slot, :, :] = part[0:ROWS]
        sib_out[slot, :, :] = part[ROWS:].astype(BF16)
        sib[mask] = links.copy(sib_out.at[slot], sib_in.at[slot], sibling, TO_CORE)

    waited = set()
    for step in STEPS:
        kind, mask = step[0], step[1]
        if step == "W7":
            weigh(14, 2, 0, WIDTH)
        elif step == "Wc":
            weigh(0, 14, 6 * LANES, WIDTH)
        elif step == "Wr":
            weigh(0, 14, 0, 6 * LANES)
        elif kind == "Q":
            query_part(int(mask))
        elif kind == "K":
            key_part(int(mask))
        elif kind == "k":
            keys.back(int(mask), int(step[2]))
        else:
            if mask not in waited:
                waited.add(mask)
                sib[int(mask)].wait_recv()
            queries.back(int(mask), int(step[2]))

    terms = 0.5 * jnp.sum(jnp.log(sums_of_rows[0][0:1, :])) + 0.5 * jnp.sum(jnp.log(sums_of_cols[0])) - positive
    loss_core[core, :, :] = jnp.broadcast_to(terms, (8, LANES))
    loss_swap = links.copy(loss_core.at[core], loss_core.at[core], sibling, LOSS_SWAP)
    loss_swap.wait_recv()
    loss_plane[place, :, :] = jnp.sum(loss_core[...], axis=0)
    sib[0].wait_recv()

    for view, group in ((1, keys), (0, queries)):
        here = slice(view * ROWS, (view + 1) * ROWS)
        gradient = SCALE * (group.whole() - pos[here, :])
        normal = unit[here, :]
        along = jnp.sum(normal * gradient, axis=1, keepdims=True)
        gm[here, :] = (inv[here, 0:1] * (gradient - normal * along)).astype(BF16)
        small = nt(gm[here, :], up_ref[...])
        gl[here, :] = small.astype(BF16)
        small_rows = small.T.astype(BF16)
        for first in range(0, TOTAL, WIDTH):
            columns = slice(first, first + WIDTH)
            value = nn(small_rows, h[here, columns]) if first < MODEL else tn(low[here, :], gm[here, :])
            if view == 0:
                value = value + gsum[:, columns]
                gsend[:, columns] = value.astype(BF16)
            gsum[:, columns] = value

    mine = pl.ds(pl.multiple_of(core * HALF_RANK, HALF_RANK), HALF_RANK)
    theirs = pl.ds(pl.multiple_of((1 - core) * HALF_RANK, HALF_RANK), HALF_RANK)
    core_got = links.copy(gsend.at[theirs], core_in, sibling, CORE)
    core_got.wait_recv()
    for piece in range(16):
        top, side = (piece // 8) * 16, (piece % 8) * PIECE
        columns = slice(side, side + PIECE)
        value = gsum[pl.ds(pl.multiple_of(core * HALF_RANK + top, 16), 16), columns]
        value = value + core_in[top : top + 16, columns].astype(F32)
        plane_out[piece, :, :] = value.astype(BF16)
    plane_slot, loss_slot = links.slot(), links.slot()
    for (dx, dy), device in plane.items():
        there = lax.rem(x + dx, 4) * 4 + lax.rem(y + dy, 4)
        links.copy(plane_out.at[there], plane_in.at[place], device, PLANE, plane_slot)
    plane_in[place, :, :] = plane_out[place]
    stores = []
    for view, target in enumerate((g1_hbm, g2_hbm)):
        here = slice(view * ROWS, (view + 1) * ROWS)
        state[view, :, 0:WIDTH] = (nn(gl[here, :], down[:, 0:WIDTH]) + gm[here, :].astype(F32)).astype(BF16)

        def chunk(step, carry, here=here, view=view):
            columns = pl.ds(pl.multiple_of(WIDTH + step * 512, 512), 512)
            state[view, :, columns] = nn(gl[here, :], down[:, columns]).astype(BF16)
            return carry

        lax.fori_loop(0, (MODEL - WIDTH) // 512, chunk, 0)
        stores.append(pltpu.make_async_copy(state.at[view], target, load_sems.at[view]))
        stores[-1].start()
    for device in plane.values():
        links.copy(loss_plane.at[place], loss_plane.at[place], device, LOSS_PLANE, loss_slot)
    links.arrived(plane_slot, plane_in.at[0:15])
    z_all[z, :, :] = jnp.sum(plane_in[...].astype(F32), axis=0).astype(BF16)
    z_slot, loss_z_slot = links.slot(), links.slot()
    for device in column.values():
        links.copy(z_all.at[z], z_all.at[z], device, COLUMN, z_slot)
    links.arrived(loss_slot, loss_plane.at[0:15])
    loss_z[z, :, :] = jnp.sum(loss_plane[...], axis=0)
    for device in column.values():
        links.copy(loss_z.at[z], loss_z.at[z], device, LOSS_COLUMN, loss_z_slot)
    links.arrived(z_slot, z_all.at[0:3])
    sums[place, :, :] = jnp.sum(z_all[...].astype(F32), axis=0).astype(BF16)
    plane_back = {
        step: links.copy(sums.at[place], sums.at[place], device, PLANE_BACK) for step, device in plane.items()
    }
    core_slot = links.slot()
    links.copy(sums.at[place], sums_hbm.at[core, place], sibling, CORE_BACK, core_slot)
    links.arrived(loss_z_slot, loss_z.at[0:3])
    loss_ref[0, 0] = jnp.sum(jnp.sum(loss_z[...], axis=0)[0:1, 0:1]) * (1.0 / TEXTS) + SCALE
    for (dx, dy), copy in plane_back.items():
        copy.wait_recv()
        came = lax.rem(x + 4 - dx, 4) * 4 + lax.rem(y + 4 - dy, 4)
        links.copy(sums.at[came], sums_hbm.at[core, came], sibling, CORE_BACK, core_slot)
    stores.append(pltpu.make_async_copy(sums, sums_hbm.at[core], load_sems.at[2]))
    stores[-1].start()
    links.sent(OF_QUERIES, q_out)
    links.sent(OF_KEYS, k_out)
    links.sent(TO_CORE, sib_out)
    for batch, whole in (
        (LOSS_SWAP, loss_core.at[0]),
        (CORE, core_in),
        (PLANE, plane_in.at[0:15]),
        (LOSS_PLANE, loss_plane.at[0:15]),
        (COLUMN, z_all.at[0:3]),
        (LOSS_COLUMN, loss_z.at[0:3]),
        (PLANE_BACK, sums.at[0:15]),
        (CORE_BACK, sums),
    ):
        links.sent(batch, whole)
    links.arrived(core_slot, sums)
    for store in stores:
        store.wait()


def finish(
    loss_in, g1_in, g2_in, sums_in, loss_out, g1_out, g2_out, gdown_out, gup_out, g1, g2, sums, grad_down, grad_up, sems
):
    def copy(source, target, index):
        made = pltpu.make_async_copy(source, target, sems.at[index])
        made.start()
        return made

    first = copy(sums_in, sums, 0)
    pieces = []
    for source, buffer, target in ((g1_in, g1, g1_out), (g2_in, g2, g2_out)):
        for top in range(0, ROWS, ROWS // 4):
            here = pl.ds(top, ROWS // 4)
            pieces.append((copy(source.at[here], buffer.at[here], 1 + len(pieces)), buffer.at[here], target.at[here]))
    loss_out[0, 0] = loss_in[0, 0]
    stores = []
    first.wait()
    for rank in range(2):
        for piece in range(16):
            top, start = rank * HALF_RANK + (piece // 8) * 16, (piece % 8) * PIECE
            last = start + PIECE
            value = sums[rank, piece].astype(F32)
            rows = slice(top, top + 16)
            if last <= MODEL:
                grad_down[rows, start:last] = value
            elif start < MODEL:
                grad_down[rows, start:MODEL] = value[:, 0 : MODEL - start]
                grad_up[rows, 0 : last - MODEL] = value[:, MODEL - start :]
            else:
                grad_up[rows, start - MODEL : last - MODEL] = value
        rows = pl.ds(rank * HALF_RANK, HALF_RANK)
        stores.append(copy(grad_down.at[rows], gdown_out.at[rows], 17 + 2 * rank))
        stores.append(copy(grad_up.at[rows], gup_out.at[rows], 18 + 2 * rank))
    for index, (load, buffer, target) in enumerate(pieces):
        load.wait()
        stores.append(copy(buffer, target, 9 + index))
    for store in stores:
        store.wait()


def shards(first_pooled_view, second_pooled_view, partner, adapter_down_weight, adapter_up_weight):
    hbm = pl.BlockSpec(memory_space=pl.ANY)
    smem = pl.BlockSpec(memory_space=pltpu.SMEM)
    down_rows = adapter_down_weight.T
    loss, first_state, second_state, sums = pl.pallas_call(
        body,
        out_shape=(
            jax.ShapeDtypeStruct((1, 1), F32),
            jax.ShapeDtypeStruct((ROWS, MODEL), BF16),
            jax.ShapeDtypeStruct((ROWS, MODEL), BF16),
            jax.ShapeDtypeStruct((2, 16, 16, PIECE), BF16),
        ),
        in_specs=[hbm, hbm, hbm, hbm, hbm],
        out_specs=(smem, hbm, hbm, hbm),
        scratch_shapes=[
            pltpu.VMEM((2 * ROWS, MODEL), BF16),
            pltpu.VMEM((RANK, MODEL), BF16),
            pltpu.VMEM((RANK, WIDTH), BF16),
            pltpu.VMEM((1, ROWS), jnp.int32),
            pltpu.VMEM((2 * ROWS, WIDTH), F32),
            pltpu.VMEM((2 * ROWS, LANES), F32),
            pltpu.VMEM((2 * ROWS, RANK), BF16),
            pltpu.VMEM((16 * ROWS, WIDTH), BF16),
            pltpu.VMEM((8 * ROWS, WIDTH), BF16),
            pltpu.VMEM((16 * ROWS, 8 * ROWS), F32),
            pltpu.VMEM((16 * ROWS, LANES), F32),
            pltpu.VMEM((8, 8 * ROWS), F32),
            pltpu.VMEM((16, LANES), F32),
            pltpu.VMEM((8, LANES), F32),
            pltpu.VMEM((7, 16, LANES), F32),
            pltpu.VMEM((16, LANES), F32),
            pltpu.VMEM((7, 8, LANES), F32),
            pltpu.VMEM((16 * ROWS, 8 * ROWS), BF16),
            pltpu.VMEM((8, 8 * ROWS), F32),
            pltpu.VMEM((8, ROWS, WIDTH), F32),
            pltpu.VMEM((8 * ROWS, WIDTH), F32),
            pltpu.VMEM((8, ROWS, WIDTH), BF16),
            pltpu.VMEM((8, ROWS, WIDTH), BF16),
            pltpu.VMEM((7, ROWS, WIDTH), BF16),
            pltpu.VMEM((7, ROWS, WIDTH), BF16),
            pltpu.VMEM((7, ROWS, WIDTH), BF16),
            pltpu.VMEM((7, ROWS, WIDTH), BF16),
            pltpu.VMEM((2 * ROWS, WIDTH), F32),
            pltpu.VMEM((2 * ROWS, RANK), BF16),
            pltpu.VMEM((2 * ROWS, WIDTH), BF16),
            pltpu.VMEM((2, ROWS, MODEL), BF16),
            pltpu.VMEM((RANK, TOTAL), F32),
            pltpu.VMEM((RANK, TOTAL), BF16),
            pltpu.VMEM((HALF_RANK, TOTAL), BF16),
            pltpu.VMEM((16, 16, PIECE), BF16),
            pltpu.VMEM((16, 16, PIECE), BF16),
            pltpu.VMEM((4, 16, PIECE), BF16),
            pltpu.VMEM((16, 16, PIECE), BF16),
            pltpu.VMEM((2, 8, LANES), F32),
            pltpu.VMEM((16, 8, LANES), F32),
            pltpu.VMEM((4, 8, LANES), F32),
            pltpu.SemaphoreType.DMA((5,)),
            pltpu.SemaphoreType.DMA((SENDS,)),
            pltpu.SemaphoreType.DMA((ARRIVALS,)),
        ],
        compiler_params=pltpu.CompilerParams(
            collective_id=0, has_side_effects=True, vmem_limit_bytes=60 * 1024 * 1024
        ),
    )(first_pooled_view, second_pooled_view, partner, down_rows, adapter_up_weight)
    loss, first_gradient, second_gradient, grad_down, grad_up = pl.pallas_call(
        finish,
        out_shape=(
            jax.ShapeDtypeStruct((1, 1), F32),
            jax.ShapeDtypeStruct((ROWS, MODEL), BF16),
            jax.ShapeDtypeStruct((ROWS, MODEL), BF16),
            jax.ShapeDtypeStruct((RANK, MODEL), F32),
            jax.ShapeDtypeStruct((RANK, WIDTH), F32),
        ),
        in_specs=[smem, hbm, hbm, hbm],
        out_specs=(smem, hbm, hbm, hbm, hbm),
        scratch_shapes=[
            pltpu.VMEM((ROWS, MODEL), BF16),
            pltpu.VMEM((ROWS, MODEL), BF16),
            pltpu.VMEM((2, 16, 16, PIECE), BF16),
            pltpu.VMEM((RANK, MODEL), F32),
            pltpu.VMEM((RANK, WIDTH), F32),
            pltpu.SemaphoreType.DMA((21,)),
        ],
        compiler_params=pltpu.CompilerParams(vmem_limit_bytes=60 * 1024 * 1024),
    )(loss, first_state, second_state, sums)
    return (loss[0, 0], first_gradient, second_gradient, grad_down.T, grad_up)


def solution(mesh):
    in_specs = (P(("blk", "grp"), None), P(("blk", "grp"), None), P(("blk", "grp"), None), P(), P())
    out_specs = (P(), P(("blk", "grp"), None), P(("blk", "grp"), None), P(), P())
    return jax.shard_map(shards, mesh=mesh, in_specs=in_specs, out_specs=out_specs, check_vma=False)
```

```python
import jax
import jax.numpy as jnp
from jax import lax
from jax.experimental import pallas as pl
from jax.experimental.pallas import tpu as pltpu
from jax.sharding import PartitionSpec as P

SCALE = 20.0
EPS = 1e-06
MESH = pl.DeviceIdType.MESH
F32 = jnp.float32
BF16 = jnp.bfloat16

ROWS = 128
WIDTH = 1024
MODEL = 4096
RANK = 64
LANES = 128
TEXTS = 16384

ORDER = (0, 1, 2, 4, 3, 6, 5, 7)
SLOT = {mask: slot for slot, mask in enumerate(ORDER)}
BACK = {(7, 0): 1, (7, 1): 4}
BACK.update({(mask, half): link for mask, link in ((6, 2), (3, 1), (5, 4), (1, 1), (2, 2), (4, 4)) for half in (0, 1)})
AFTER = {(6, 0): 7, (3, 1): 7}
AFTER.update({(mask, half): add for mask, add in ((1, 5), (2, 3), (4, 6)) for half in (0, 1)})
STEPS = (
    "W7", "Q7", "Wc", "Wr", "Q5", "q70", "q71", "K7", "k71", "k70", "Q3", "Q6", "K6", "k61", "q51", "K3", "q30",
    "k30", "K5", "k51", "K0", "q60", "q50", "q61", "K4", "q31", "k31", "k60", "k50", "Q2", "Q1", "Q4", "K2", "k41",
    "K1", "k20", "q11", "q20", "k11", "q40", "q21", "k10", "q10", "k40", "k21", "q41", "Q0",
)
SPANS = {"low": (0, 64), "high": (64, 128), "mid": (32, 96), "bottom": (0, 32), "top": (96, 128)}
SPANS.update({"first": (0, 48), "second": (48, 80), "third": (80, 128)})
TURNS = {4: (("low",), ("high",)), 2: (("high",), ("low",)), 1: (("mid",), ("bottom", "top"))}
NEXT = {4: 2, 2: 1, 1: 4}
CORNER = ((6, 4, "first", 1), (3, 2, "third", 4), (5, 1, "second", 2))
HALF = ROWS // 2
SENDS, ARRIVALS = 14, 98
OF_QUERIES, OF_KEYS, TO_CORE, OF_ROWS, OF_COLS, ROW_SWAP, CORE, PLANE, LOSS_PLANE, COLUMN, LOSS_COLUMN, PLANE_BACK, CORE_BACK, LOSS_SWAP = range(SENDS)
TOTAL = MODEL + WIDTH
HALF_RANK = RANK // 2
PIECE = TOTAL // 8


def nn(a, b):
    return lax.dot_general(a, b, (((1,), (0,)), ((), ())), preferred_element_type=F32)


def nt(a, b):
    return lax.dot_general(a, b, (((1,), (1,)), ((), ())), preferred_element_type=F32)


def tn(a, b):
    return lax.dot_general(a, b, (((0,), (0,)), ((), ())), preferred_element_type=F32)


class Links:
    def __init__(self, send_sems, recv_sems, device):
        self.send_sems, self.recv_sems, self.device, self.count = send_sems, recv_sems, device, 0

    def slot(self):
        self.count += 1
        return self.count - 1

    def make(self, src, dst, device, batch, slot):
        return pltpu.make_async_remote_copy(
            src_ref=src,
            dst_ref=dst,
            send_sem=self.send_sems.at[batch],
            recv_sem=self.recv_sems.at[slot],
            device_id=device,
            device_id_type=MESH,
        )

    def copy(self, src, dst, device, batch, slot=None):
        made = self.make(src, dst, device, batch, self.slot() if slot is None else slot)
        made.start()
        return made

    def sent(self, batch, whole):
        self.make(whole, whole, self.device, batch, 0).wait_send()

    def arrived(self, slot, whole):
        self.make(whole, whole, self.device, 0, slot).wait_recv()


def half_rows(half):
    return slice(half * HALF, (half + 1) * HALF)


class Group:
    def __init__(self, links, near, data, stride, out, landing, part, ready, batch):
        self.links, self.near, self.data, self.stride, self.ready, self.batch = links, near, data, stride, ready, batch
        self.out, self.landing, self.part, self.got, self.back_got = out, landing, part, {}, {}

    def at(self, mask, part):
        first, last = SPANS[part]
        return self.data.at[SLOT[mask] * self.stride + first : SLOT[mask] * self.stride + last]

    def give(self, mask, part, link):
        there = mask ^ link
        self.got[there, part] = self.links.copy(self.at(mask, part), self.at(there, part), self.near[link], self.batch)

    def have(self, mask, part):
        self.got[mask, part].wait_recv()

    def back(self, mask, half):
        rows, add = half_rows(half), AFTER.get((mask, half))
        if add is not None:
            self.back_got[add, half].wait_recv()
            value = self.part(mask, rows) + self.landing[add - 1, rows].astype(F32)
            self.out[mask - 1, rows] = value.astype(BF16)
        elif not self.ready:
            self.out[mask - 1, rows] = self.part(mask, rows).astype(BF16)
        self.back_got[mask, half] = self.links.copy(
            self.out.at[mask - 1, rows], self.landing.at[mask - 1, rows], self.near[BACK[mask, half]], self.batch
        )

    def whole(self):
        total = self.part(0, slice(0, ROWS))
        for mask in (1, 2, 4):
            for half in (0, 1):
                self.back_got[mask, half].wait_recv()
        for mask in (1, 2, 4):
            total = total + self.landing[mask - 1].astype(F32)
        return total


def body(
    h1_hbm, h2_hbm, partner_hbm, down_hbm, up_hbm,
    loss_ref, g1_hbm, g2_hbm, sums_hbm,
    h, down, up_ref, partner_ref, unit, inv, low, q, k, expo, rowacc, colacc, rows, cols, row_in, row_sib_in, col_in,
    w, colb, pq, pk, sib_out, sib_in, q_out, q_in, k_out, k_in, pos,
    gl, gm, state, gsum, gsend, core_in, plane_out, plane_in, z_all, sums,
    loss_core, loss_plane, loss_z,
    load_sems, send_sems, recv_sems,
):
    blk, grp = lax.axis_index("blk"), lax.axis_index("grp")
    x, z_hi = lax.div(blk, 2), lax.rem(blk, 2)
    z_lo, y, core = lax.div(grp, 8), lax.rem(lax.div(grp, 2), 4), lax.rem(grp, 2)
    z = z_hi * 2 + z_lo
    place = x * 4 + y

    def at(dx=0, dy=0, dz=0, other=False):
        px, py, pz = lax.rem(x + dx, 4), lax.rem(y + dy, 4), lax.rem(z + dz, 4)
        pc = 1 - core if other else core
        return (px * 2 + lax.div(pz, 2), lax.rem(pz, 2) * 8 + py * 2 + pc)

    up_or_down = [1 + 2 * lax.rem(c, 2) for c in (x, y, z)]

    def cube(flip):
        steps = [4 - s if flip else s for s in up_or_down]
        return {m: at(*(s if m & bit else 0 for bit, s in zip((1, 2, 4), steps))) for m in range(1, 8)}

    sibling = at(other=True)
    q_near, k_near = cube(False), cube(True)
    far_first = sorted(((dx, dy) for dx in range(4) for dy in range(4) if dx or dy), key=lambda d: -sum(min(c, 4 - c) for c in d))
    plane = {step: at(*step) for step in far_first}
    column = {dz: at(dz=dz) for dz in (1, 2, 3)}
    links = Links(send_sems, recv_sems, sibling)

    loads = [
        pltpu.make_async_copy(down_hbm, down, load_sems.at[2]),
        pltpu.make_async_copy(h1_hbm, h.at[0:ROWS], load_sems.at[0]),
        pltpu.make_async_copy(up_hbm, up_ref, load_sems.at[3]),
        pltpu.make_async_copy(h2_hbm, h.at[ROWS : 2 * ROWS], load_sems.at[1]),
        pltpu.make_async_copy(partner_hbm, partner_ref, load_sems.at[4]),
    ]
    for load in loads:
        load.start()
    partners = [sibling, *(near[m] for near in (q_near, k_near) for m in (1, 2, 4))]
    barrier = pltpu.get_barrier_semaphore()
    for device in partners:
        pl.semaphore_signal(barrier, inc=1, device_id=device, device_id_type=MESH)
    rowacc[...] = jnp.zeros_like(rowacc)
    colacc[...] = jnp.zeros_like(colacc)

    for view, own in enumerate((q, k)):
        here = slice(view * ROWS, (view + 1) * ROWS)
        for load in loads[3 * view : 3 * view + 3]:
            load.wait()
        low[here, :] = nt(h[here, :], down[...]).astype(BF16)
        mixed = h[here, 0:WIDTH].astype(F32) + nn(low[here, :], up_ref[...])
        inverse = lax.rsqrt(jnp.sum(mixed * mixed, axis=1, keepdims=True) + EPS)
        inv[here, :] = jnp.broadcast_to(inverse, (ROWS, LANES))
        normal = mixed * inverse
        unit[here, :] = normal
        own[0:ROWS, :] = normal.astype(BF16)
    pl.semaphore_wait(barrier, len(partners))

    sib = {}

    def q_part(mask, here):
        return pq[SLOT[mask], here, :] + sib_in[SLOT[mask], here, :].astype(F32)

    def k_part(mask, here):
        first = SLOT[mask] * ROWS
        return pk[first + here.start : first + here.stop, :]

    queries = Group(links, q_near, q, 2 * ROWS, q_out, q_in, q_part, False, OF_QUERIES)
    keys = Group(links, k_near, k, ROWS, k_out, k_in, k_part, True, OF_KEYS)
    groups = (queries, keys)

    BATCH = {0: 0, 1: 0, 2: 0, 4: 0, 3: 1, 6: 1, 5: 1, 7: 2}
    core_slots = [links.slot() for _ in range(3)]

    def to_sibling(mask, first, last):
        top = SLOT[mask] * 2 * ROWS
        here, there = q.at[top + first : top + last], q.at[top + ROWS + first : top + ROWS + last]
        links.copy(here, there, sibling, TO_CORE, core_slots[BATCH[mask]])

    def sibling_has(batch, shards_of):
        links.arrived(core_slots[batch], q.at[0 : shards_of * ROWS])

    for turn in (0, 1):
        for group in groups:
            for link in (4, 2, 1):
                for part in TURNS[link][turn]:
                    group.give(0, part, link)
    to_sibling(0, 0, ROWS)
    for turn in (0, 1):
        for group in groups:
            for mask in (4, 2, 1):
                for part in TURNS[mask][turn]:
                    group.have(mask, part)
                    group.give(mask, part, NEXT[mask])
                    if group is queries:
                        to_sibling(mask, *SPANS[part])

    def score(first_row, row_count, first_col, col_count):
        columns = slice(first_col, first_col + col_count)
        for top in range(first_row, first_row + row_count, 512):
            here = slice(top, min(top + 512, first_row + row_count))
            value = jnp.exp(SCALE * nt(q[here, :], k[columns, :]) - SCALE)
            expo[here, columns] = value
            colacc[:, columns] += jnp.sum(value.reshape(-1, 8, col_count), axis=0)
            total = value[:, 0:LANES]
            for lane in range(LANES, col_count, LANES):
                total = total + value[:, lane : lane + LANES]
            rowacc[here, :] += total

    sibling_has(0, 4)
    score(0, 1024, 0, 512)
    for turn in (0, 1):
        for group in groups:
            for mask, kind, corner, link in CORNER:
                for part in TURNS[kind][turn]:
                    group.have(mask, part)
                    if group is queries:
                        to_sibling(mask, *SPANS[part])
                if turn == 0:
                    group.give(mask, corner, link)
    score(0, 1024, 512, 256)
    sibling_has(1, 3)
    score(1024, 768, 0, 768)
    for corner in ("first", "second", "third"):
        queries.have(7, corner)
        to_sibling(7, *SPANS[corner])
    for corner in ("first", "second", "third"):
        keys.have(7, corner)
    score(0, 1792, 768, 256)
    sibling_has(2, 1)
    score(1792, 256, 0, 1024)
    links.sent(OF_QUERIES, q.at[0 : 7 * ROWS])
    links.sent(OF_KEYS, k.at[0 : 7 * ROWS])
    links.sent(TO_CORE, q.at[0 : 8 * ROWS])


    for block in range(8):
        cols[block : block + 1, :] = jnp.sum(colacc[:, block * LANES : (block + 1) * LANES], axis=0, keepdims=True)
    col_slot = links.slot()
    for m in (7, 6, 5, 3, 4, 2, 1):
        links.copy(cols, col_in.at[m - 1], k_near[m], OF_COLS, col_slot)
    for block in range(16):
        lanes = rowacc[block * ROWS : (block + 1) * ROWS, :].T
        rows[block : block + 1, :] = jnp.sum(lanes, axis=0, keepdims=True)
    row_swap = links.copy(rows, row_sib_in, sibling, ROW_SWAP)
    row_swap.wait()
    for slot in range(8):
        for rank in range(2):
            here, there = slot * 2 + rank, slot * 2 + 1 - rank
            rows[here : here + 1, :] = rows[here : here + 1, :] + row_sib_in[there : there + 1, :]
    row_slot = links.slot()
    for m in (7, 6, 5, 3, 4, 2, 1):
        links.copy(rows, row_in.at[m - 1], q_near[m], OF_ROWS, row_slot)

    choice = (lax.broadcasted_iota(jnp.int32, (ROWS, ROWS), 0) == partner_ref[...]).astype(BF16)
    pos[0:ROWS, :] = tn(choice, k[0:ROWS, :])
    pos[ROWS : 2 * ROWS, :] = nn(choice, q[0:ROWS, :])
    positive = SCALE * jnp.sum(q[0:ROWS, :].astype(F32) * pos[0:ROWS, :])

    def cube_sum(total, arrived, batch, slot, width):
        links.arrived(slot, arrived)
        links.sent(batch, arrived)
        sums = []
        for mask in ORDER:
            value = total[SLOT[mask] * width : (SLOT[mask] + 1) * width, :]
            for m in range(1, 8):
                there = SLOT[mask ^ m] * width
                value = value + arrived[m - 1, there : there + width, :]
            sums.append(value)
        return sums

    sums_of_cols = cube_sum(cols, col_in, OF_COLS, col_slot, 1)
    for slot, value in enumerate(sums_of_cols):
        colb[0:1, slot * LANES : (slot + 1) * LANES] = 0.5 / value
    sums_of_rows = cube_sum(rows, row_in, OF_ROWS, row_slot, 2)
    for slot, value in enumerate(sums_of_rows):
        half = 0.5 / value
        for rank in range(2):
            first = (2 * slot + rank) * ROWS
            rowacc[first : first + ROWS, :] = jnp.broadcast_to(half[rank : rank + 1, :], (ROWS, LANES)).T

    def weigh(first_block, count, first_lane, last_lane):
        def blocks(step, carry):
            for part in range(2):
                block = first_block + step * 2 + part
                here = pl.ds(pl.multiple_of(block * ROWS, ROWS), ROWS)
                row = rowacc[here, :]
                for lane in range(first_lane, last_lane, LANES):
                    columns = slice(lane, lane + LANES)
                    w[here, columns] = (expo[here, columns] * (row + colb[0:1, columns])).astype(BF16)
            return carry

        lax.fori_loop(0, count // 2, blocks, 0)

    def key_part(mask):
        first = SLOT[mask] * ROWS
        value = tn(w[:, first : first + ROWS], q[...])
        for half in (0, 1):
            here = half_rows(half)
            if mask and (mask, half) not in AFTER:
                k_out[mask - 1, here, :] = value[here].astype(BF16)
            else:
                pk[first + here.start : first + here.stop, :] = value[here]

    def query_part(mask):
        slot = SLOT[mask]
        here = slot * 2 * ROWS
        part = nn(w[here : here + 2 * ROWS, :], k[...])
        pq[slot, :, :] = part[0:ROWS]
        sib_out[slot, :, :] = part[ROWS:].astype(BF16)
        sib[mask] = links.copy(sib_out.at[slot], sib_in.at[slot], sibling, TO_CORE)

    waited = set()
    for step in STEPS:
        kind, mask = step[0], step[1]
        if step == "W7":
            weigh(14, 2, 0, WIDTH)
        elif step == "Wc":
            weigh(0, 14, 6 * LANES, WIDTH)
        elif step == "Wr":
            weigh(0, 14, 0, 6 * LANES)
        elif kind == "Q":
            query_part(int(mask))
        elif kind == "K":
            key_part(int(mask))
        elif kind == "k":
            keys.back(int(mask), int(step[2]))
        else:
            if mask not in waited:
                waited.add(mask)
                sib[int(mask)].wait_recv()
            queries.back(int(mask), int(step[2]))

    terms = 0.5 * jnp.sum(jnp.log(sums_of_rows[0][0:1, :])) + 0.5 * jnp.sum(jnp.log(sums_of_cols[0])) - positive
    loss_core[core, :, :] = jnp.broadcast_to(terms, (8, LANES))
    loss_swap = links.copy(loss_core.at[core], loss_core.at[core], sibling, LOSS_SWAP)
    loss_swap.wait_recv()
    loss_plane[place, :, :] = jnp.sum(loss_core[...], axis=0)
    sib[0].wait_recv()

    for view, group in ((1, keys), (0, queries)):
        here = slice(view * ROWS, (view + 1) * ROWS)
        gradient = SCALE * (group.whole() - pos[here, :])
        normal = unit[here, :]
        along = jnp.sum(normal * gradient, axis=1, keepdims=True)
        gm[here, :] = (inv[here, 0:1] * (gradient - normal * along)).astype(BF16)
        small = nt(gm[here, :], up_ref[...])
        gl[here, :] = small.astype(BF16)
        small_rows = small.T.astype(BF16)
        for first in range(0, TOTAL, WIDTH):
            columns = slice(first, first + WIDTH)
            value = nn(small_rows, h[here, columns]) if first < MODEL else tn(low[here, :], gm[here, :])
            if view == 0:
                value = value + gsum[:, columns]
                gsend[:, columns] = value.astype(BF16)
            gsum[:, columns] = value

    mine = pl.ds(pl.multiple_of(core * HALF_RANK, HALF_RANK), HALF_RANK)
    theirs = pl.ds(pl.multiple_of((1 - core) * HALF_RANK, HALF_RANK), HALF_RANK)
    core_got = links.copy(gsend.at[theirs], core_in, sibling, CORE)
    core_got.wait_recv()
    for piece in range(16):
        top, side = (piece // 8) * 16, (piece % 8) * PIECE
        columns = slice(side, side + PIECE)
        value = gsum[pl.ds(pl.multiple_of(core * HALF_RANK + top, 16), 16), columns]
        value = value + core_in[top : top + 16, columns].astype(F32)
        plane_out[piece, :, :] = value.astype(BF16)
    plane_slot, loss_slot = links.slot(), links.slot()
    for (dx, dy), device in plane.items():
        there = lax.rem(x + dx, 4) * 4 + lax.rem(y + dy, 4)
        links.copy(plane_out.at[there], plane_in.at[place], device, PLANE, plane_slot)
    plane_in[place, :, :] = plane_out[place]
    stores = []
    for view, target in enumerate((g1_hbm, g2_hbm)):
        here = slice(view * ROWS, (view + 1) * ROWS)
        state[view, :, 0:WIDTH] = (nn(gl[here, :], down[:, 0:WIDTH]) + gm[here, :].astype(F32)).astype(BF16)

        def chunk(step, carry, here=here, view=view):
            columns = pl.ds(pl.multiple_of(WIDTH + step * 512, 512), 512)
            state[view, :, columns] = nn(gl[here, :], down[:, columns]).astype(BF16)
            return carry

        lax.fori_loop(0, (MODEL - WIDTH) // 512, chunk, 0)
        stores.append(pltpu.make_async_copy(state.at[view], target, load_sems.at[view]))
        stores[-1].start()
    for device in plane.values():
        links.copy(loss_plane.at[place], loss_plane.at[place], device, LOSS_PLANE, loss_slot)
    links.arrived(plane_slot, plane_in.at[0:15])
    z_all[z, :, :] = jnp.sum(plane_in[...].astype(F32), axis=0).astype(BF16)
    z_slot, loss_z_slot = links.slot(), links.slot()
    for device in column.values():
        links.copy(z_all.at[z], z_all.at[z], device, COLUMN, z_slot)
    links.arrived(loss_slot, loss_plane.at[0:15])
    loss_z[z, :, :] = jnp.sum(loss_plane[...], axis=0)
    for device in column.values():
        links.copy(loss_z.at[z], loss_z.at[z], device, LOSS_COLUMN, loss_z_slot)
    links.arrived(z_slot, z_all.at[0:3])
    sums[place, :, :] = jnp.sum(z_all[...].astype(F32), axis=0).astype(BF16)
    plane_back = {
        step: links.copy(sums.at[place], sums.at[place], device, PLANE_BACK) for step, device in plane.items()
    }
    core_slot = links.slot()
    links.copy(sums.at[place], sums_hbm.at[core, place], sibling, CORE_BACK, core_slot)
    links.arrived(loss_z_slot, loss_z.at[0:3])
    loss_ref[0, 0] = jnp.sum(jnp.sum(loss_z[...], axis=0)[0:1, 0:1]) * (1.0 / TEXTS) + SCALE
    for (dx, dy), copy in plane_back.items():
        copy.wait_recv()
        came = lax.rem(x + 4 - dx, 4) * 4 + lax.rem(y + 4 - dy, 4)
        links.copy(sums.at[came], sums_hbm.at[core, came], sibling, CORE_BACK, core_slot)
    stores.append(pltpu.make_async_copy(sums, sums_hbm.at[core], load_sems.at[2]))
    stores[-1].start()
    links.sent(OF_QUERIES, q_out)
    links.sent(OF_KEYS, k_out)
    links.sent(TO_CORE, sib_out)
    for batch, whole in (
        (LOSS_SWAP, loss_core.at[0]),
        (CORE, core_in),
        (PLANE, plane_in.at[0:15]),
        (LOSS_PLANE, loss_plane.at[0:15]),
        (COLUMN, z_all.at[0:3]),
        (LOSS_COLUMN, loss_z.at[0:3]),
        (PLANE_BACK, sums.at[0:15]),
        (CORE_BACK, sums),
    ):
        links.sent(batch, whole)
    links.arrived(core_slot, sums)
    for store in stores:
        store.wait()


def finish(
    loss_in, g1_in, g2_in, sums_in, loss_out, g1_out, g2_out, gdown_out, gup_out, g1, g2, sums, grad_down, grad_up, sems
):
    def copy(source, target, index):
        made = pltpu.make_async_copy(source, target, sems.at[index])
        made.start()
        return made

    first = copy(sums_in, sums, 0)
    pieces = []
    for source, buffer, target in ((g1_in, g1, g1_out), (g2_in, g2, g2_out)):
        for top in range(0, ROWS, ROWS // 4):
            here = pl.ds(top, ROWS // 4)
            pieces.append((copy(source.at[here], buffer.at[here], 1 + len(pieces)), buffer.at[here], target.at[here]))
    loss_out[0, 0] = loss_in[0, 0]
    stores = []
    first.wait()
    for rank in range(2):
        for piece in range(16):
            top, start = rank * HALF_RANK + (piece // 8) * 16, (piece % 8) * PIECE
            last = start + PIECE
            value = sums[rank, piece].astype(F32)
            rows = slice(top, top + 16)
            if last <= MODEL:
                grad_down[rows, start:last] = value
            elif start < MODEL:
                grad_down[rows, start:MODEL] = value[:, 0 : MODEL - start]
                grad_up[rows, 0 : last - MODEL] = value[:, MODEL - start :]
            else:
                grad_up[rows, start - MODEL : last - MODEL] = value
        rows = pl.ds(rank * HALF_RANK, HALF_RANK)
        stores.append(copy(grad_down.at[rows], gdown_out.at[rows], 17 + 2 * rank))
        stores.append(copy(grad_up.at[rows], gup_out.at[rows], 18 + 2 * rank))
    for index, (load, buffer, target) in enumerate(pieces):
        load.wait()
        stores.append(copy(buffer, target, 9 + index))
    for store in stores:
        store.wait()


def shards(first_pooled_view, second_pooled_view, partner, adapter_down_weight, adapter_up_weight):
    hbm = pl.BlockSpec(memory_space=pl.ANY)
    smem = pl.BlockSpec(memory_space=pltpu.SMEM)
    down_rows = adapter_down_weight.T
    loss, first_state, second_state, sums = pl.pallas_call(
        body,
        out_shape=(
            jax.ShapeDtypeStruct((1, 1), F32),
            jax.ShapeDtypeStruct((ROWS, MODEL), BF16),
            jax.ShapeDtypeStruct((ROWS, MODEL), BF16),
            jax.ShapeDtypeStruct((2, 16, 16, PIECE), BF16),
        ),
        in_specs=[hbm, hbm, hbm, hbm, hbm],
        out_specs=(smem, hbm, hbm, hbm),
        scratch_shapes=[
            pltpu.VMEM((2 * ROWS, MODEL), BF16),
            pltpu.VMEM((RANK, MODEL), BF16),
            pltpu.VMEM((RANK, WIDTH), BF16),
            pltpu.VMEM((1, ROWS), jnp.int32),
            pltpu.VMEM((2 * ROWS, WIDTH), F32),
            pltpu.VMEM((2 * ROWS, LANES), F32),
            pltpu.VMEM((2 * ROWS, RANK), BF16),
            pltpu.VMEM((16 * ROWS, WIDTH), BF16),
            pltpu.VMEM((8 * ROWS, WIDTH), BF16),
            pltpu.VMEM((16 * ROWS, 8 * ROWS), F32),
            pltpu.VMEM((16 * ROWS, LANES), F32),
            pltpu.VMEM((8, 8 * ROWS), F32),
            pltpu.VMEM((16, LANES), F32),
            pltpu.VMEM((8, LANES), F32),
            pltpu.VMEM((7, 16, LANES), F32),
            pltpu.VMEM((16, LANES), F32),
            pltpu.VMEM((7, 8, LANES), F32),
            pltpu.VMEM((16 * ROWS, 8 * ROWS), BF16),
            pltpu.VMEM((8, 8 * ROWS), F32),
            pltpu.VMEM((8, ROWS, WIDTH), F32),
            pltpu.VMEM((8 * ROWS, WIDTH), F32),
            pltpu.VMEM((8, ROWS, WIDTH), BF16),
            pltpu.VMEM((8, ROWS, WIDTH), BF16),
            pltpu.VMEM((7, ROWS, WIDTH), BF16),
            pltpu.VMEM((7, ROWS, WIDTH), BF16),
            pltpu.VMEM((7, ROWS, WIDTH), BF16),
            pltpu.VMEM((7, ROWS, WIDTH), BF16),
            pltpu.VMEM((2 * ROWS, WIDTH), F32),
            pltpu.VMEM((2 * ROWS, RANK), BF16),
            pltpu.VMEM((2 * ROWS, WIDTH), BF16),
            pltpu.VMEM((2, ROWS, MODEL), BF16),
            pltpu.VMEM((RANK, TOTAL), F32),
            pltpu.VMEM((RANK, TOTAL), BF16),
            pltpu.VMEM((HALF_RANK, TOTAL), BF16),
            pltpu.VMEM((16, 16, PIECE), BF16),
            pltpu.VMEM((16, 16, PIECE), BF16),
            pltpu.VMEM((4, 16, PIECE), BF16),
            pltpu.VMEM((16, 16, PIECE), BF16),
            pltpu.VMEM((2, 8, LANES), F32),
            pltpu.VMEM((16, 8, LANES), F32),
            pltpu.VMEM((4, 8, LANES), F32),
            pltpu.SemaphoreType.DMA((5,)),
            pltpu.SemaphoreType.DMA((SENDS,)),
            pltpu.SemaphoreType.DMA((ARRIVALS,)),
        ],
        compiler_params=pltpu.CompilerParams(
            collective_id=0, has_side_effects=True, vmem_limit_bytes=60 * 1024 * 1024
        ),
    )(first_pooled_view, second_pooled_view, partner, down_rows, adapter_up_weight)
    loss, first_gradient, second_gradient, grad_down, grad_up = pl.pallas_call(
        finish,
        out_shape=(
            jax.ShapeDtypeStruct((1, 1), F32),
            jax.ShapeDtypeStruct((ROWS, MODEL), BF16),
            jax.ShapeDtypeStruct((ROWS, MODEL), BF16),
            jax.ShapeDtypeStruct((RANK, MODEL), F32),
            jax.ShapeDtypeStruct((RANK, WIDTH), F32),
        ),
        in_specs=[smem, hbm, hbm, hbm],
        out_specs=(smem, hbm, hbm, hbm, hbm),
        scratch_shapes=[
            pltpu.VMEM((ROWS, MODEL), BF16),
            pltpu.VMEM((ROWS, MODEL), BF16),
            pltpu.VMEM((2, 16, 16, PIECE), BF16),
            pltpu.VMEM((RANK, MODEL), F32),
            pltpu.VMEM((RANK, WIDTH), F32),
            pltpu.SemaphoreType.DMA((21,)),
        ],
        compiler_params=pltpu.CompilerParams(vmem_limit_bytes=60 * 1024 * 1024),
    )(loss, first_state, second_state, sums)
    return (loss[0, 0], first_gradient, second_gradient, grad_down.T, grad_up)


def solution(mesh):
    in_specs = (P(("blk", "grp"), None), P(("blk", "grp"), None), P(("blk", "grp"), None), P(), P())
    out_specs = (P(), P(("blk", "grp"), None), P(("blk", "grp"), None), P(), P())
    return jax.shard_map(shards, mesh=mesh, in_specs=in_specs, out_specs=out_specs, check_vma=False)
```
